512 devices in a mesh: ao: 64 (over y, z), grp: 8 (over x, core).
Axes of the slice: x: 4, y: 4, z: 16, core: 2. Of those that a mesh axis runs over, the one named last changes fastest.
Arguments:
- three_center: bfloat16 [8, 512, 28672], P(None, 'grp', 'ao'), may hold values from -6 to 6
- occ_density: bfloat16 [8, 64, 64, 448], P('grp', 'ao'), may hold values from -0.25 to 0.25
- virt_density: bfloat16 [8, 64, 64, 448], P('grp', 'ao'), may hold values from -0.25 to 0.25
- tensor_mask: int32 [8, 64, 7], replicated, may hold values 0 or 1
- occ_mask: int32 [8, 64, 7], replicated, may hold values 0 or 1
- virt_mask: int32 [8, 64, 7], replicated, may hold values 0 or 1
- block_sizes: int32 [8, 64], replicated, may hold values from 32 to 64
Outputs:
- polarizability: float32 [8, 8], P('grp')
The draws below stay inside these ranges and needn't reach their ends.
All inputs are finite; a program needn't handle non-finite values.
Results may differ from the reference program's by a relative error of at most 0.0043.
Values may be sent and summed in bfloat16 or wider, within the bound.
A program may use at most 64 MiB of HBM per device.

```python
import math
import jax
import jax.numpy as jnp
from jax import lax

BS = 64
PLANE_ROWS = 4
RI = 8
LINE = 16
NB = 512
N_AO = 64
N_GRP = 8


def touch_ends(result, rng, low, largest):
    spot = [jax.random.randint(jax.random.fold_in(rng, axis), (), 0, length) for axis, length in enumerate(result.shape)]
    longest = result.shape.index(max(result.shape))
    beside = spot[:longest] + [(spot[longest] + 1) % result.shape[longest]] + spot[longest + 1:]
    return result.at[tuple(spot)].set(low).at[tuple(beside)].set(largest)


def raised(values, rng, source, target, parts, factor):
    def block_of(dim):
        return (jnp.arange(values.shape[dim]) // (values.shape[dim] // parts)).reshape((-1,) + (1,) * (values.ndim - 1 - dim))

    first = jax.random.permutation(rng, parts)[block_of(target)]
    second = (block_of(target) + parts // 2) % parts
    return jnp.where((block_of(source) == first) | (block_of(source) == second), factor * values, values)


def shard_levels(key, extent, shards, low, top_value):
    factor_of, own = 1.0, jax.random.fold_in(key, 6)
    for axis_at, blocks in shards:
        draws = jnp.exp(jax.random.uniform(jax.random.fold_in(own, axis_at), (blocks,), jnp.float32, low / len(shards), top_value / len(shards)))
        factor_of = factor_of * jnp.repeat(draws, extent[axis_at] // blocks).reshape([-1 if axis == axis_at else 1 for axis in range(len(extent))])
    return factor_of


def noise(own_key, extent, scale, limit, cuts=(), kind=jnp.bfloat16):
    array = scale * jax.random.normal(own_key, extent, jnp.float32)
    if cuts:
        array = array * shard_levels(own_key, extent, cuts, -0.22, 0.18)
    return jnp.clip(array, -limit, limit).astype(kind)


def gaussian_with(own_key, shape, deviation, limit, split, heavy, kind=jnp.bfloat16):
    array = deviation * jax.random.normal(own_key, shape, jnp.float32)
    if split:
        array = array * shard_levels(own_key, shape, split, -0.22, 0.18)
    return jnp.clip(raised(array, jax.random.fold_in(own_key, 3), *heavy), -limit, limit).astype(kind)


def setup_inputs(seed: int = 0) -> dict:
    seeds = jax.random.split(jax.random.key(seed), 8)
    return {
        "three_center": gaussian_with(seeds[0], (RI, NB, 7 * BS * BS), 1.0, 6.0, ((1, 8), (2, 64)), (1, 0, 8, 2.0)),
        "occ_density": noise(seeds[1], (N_GRP, N_AO, BS, 7 * BS), (7 * BS) ** -0.5, 0.25, ((0, 8), (1, 64))),
        "virt_density": noise(seeds[2], (N_GRP, N_AO, BS, 7 * BS), (7 * BS) ** -0.5, 0.25, ((0, 8), (1, 64))),
        "tensor_mask": touch_ends((jax.random.randint(seeds[3], (N_GRP, N_AO, 7), 0, 4) < 3).astype(jnp.int32), jax.random.fold_in(seeds[3], 1), 0, 1),
        "occ_mask": touch_ends((jax.random.randint(seeds[4], (N_GRP, N_AO, 7), 0, 4) < 3).astype(jnp.int32), jax.random.fold_in(seeds[4], 1), 0, 1),
        "virt_mask": touch_ends((jax.random.randint(seeds[5], (N_GRP, N_AO, 7), 0, 4) < 3).astype(jnp.int32), jax.random.fold_in(seeds[5], 1), 0, 1),
        "block_sizes": touch_ends(jax.random.randint(seeds[6], (N_GRP, N_AO), BS // 2, BS + 1), jax.random.fold_in(seeds[6], 1), BS // 2, BS).astype(jnp.int32),
    }


stencil_steps = ((0, 0, 0), (-1, 0, 0), (1, 0, 0), (0, -1, 0), (0, 1, 0), (0, 0, -1), (0, 0, 1))
reverse_step = (0, 2, 1, 4, 3, 6, 5)

def reach_table():
    found = []
    for first_step in stencil_steps:
        for second_step in stencil_steps:
            total = (first_step[0] + second_step[0], first_step[1] + second_step[1], first_step[2] + second_step[2])
            if total not in found:
                found.append(total)
    return found

def offset_between(first_step, second_step, factor):
    return (first_step[0] + factor * second_step[0], first_step[1] + factor * second_step[1], first_step[2] + factor * second_step[2])

def neighbour_table():
    blocks = jnp.arange(NB, dtype=jnp.int32)
    first_at = blocks // N_AO
    second_at = blocks % N_AO // LINE
    third_at = blocks % LINE
    columns = []
    for first_step in stencil_steps:
        first_to = first_at + first_step[0]
        second_to = second_at + first_step[1]
        third_to = third_at + first_step[2]
        inside = (first_to >= 0) & (first_to < N_GRP) & (second_to >= 0) & (second_to < PLANE_ROWS) & (third_to >= 0) & (third_to < LINE)
        columns.append(jnp.where(inside, first_to * N_AO + second_to * LINE + third_to, NB).astype(jnp.int32))
    return jnp.stack(columns, axis=1)

def mask_density(density, mask_table, sizes_ext, table):
    square = density.reshape(NB, BS, 7 * BS)
    beside = sizes_ext[table]
    valid = table < NB
    offsets = jnp.arange(BS, dtype=jnp.int32)
    column_keep = (offsets[None, None, :] < beside[:, :, None]) & (mask_table.reshape(NB, 7)[:, :, None] > 0) & valid[:, :, None]
    row_keep = offsets[None, :] < beside[:, 0:1]
    keep_both = row_keep[:, :, None] & column_keep.reshape(NB, 1, 7 * BS)
    masked = jnp.where(keep_both, square, jnp.zeros_like(square))
    return jnp.concatenate([masked, jnp.zeros((1, BS, 7 * BS), masked.dtype)])

def reference(three_center, occ_density, virt_density, tensor_mask, occ_mask, virt_mask, block_sizes):
    reach = reach_table()
    table = neighbour_table()
    sizes_ext = jnp.concatenate([block_sizes.reshape(NB).astype(jnp.int32), jnp.zeros((1,), jnp.int32)])
    occ_ext = mask_density(occ_density, occ_mask, sizes_ext, table)
    virt_ext = mask_density(virt_density, virt_mask, sizes_ext, table)
    weights = (tensor_mask.reshape(NB, 7) > 0) & (table < NB)

    def tensor_piece(block_at):
        piece = lax.dynamic_index_in_dim(three_center, block_at, 1, keepdims=False).reshape(RI, BS, 7 * BS)
        weight_row = lax.dynamic_index_in_dim(weights, block_at, 0, keepdims=False)
        keep = jnp.repeat(weight_row, BS, total_repeat_length=7 * BS)
        return jnp.where(keep[None, None, :], piece, jnp.zeros_like(piece))

    def half_block(block_at):
        tensor_rows = tensor_piece(block_at).reshape(RI * BS, 7 * BS)
        nearby = lax.dynamic_index_in_dim(table, block_at, 0, keepdims=False)
        slots = [None] * len(reach)
        for which in range(7):
            virt_row = lax.dynamic_index_in_dim(virt_ext, nearby[which], 0, keepdims=False)
            product = jnp.dot(tensor_rows[:, which * BS:(which + 1) * BS], virt_row, preferred_element_type=jnp.float32)
            for other in range(7):
                target = reach.index(offset_between(stencil_steps[which], stencil_steps[other], 1))
                portion = product[:, other * BS:(other + 1) * BS]
                slots[target] = portion if slots[target] is None else slots[target] + portion
        return jnp.concatenate(slots, axis=1).astype(jnp.bfloat16).reshape(RI, BS, len(reach) * BS)

    def half_plane(plane_at):
        return lax.map(lambda along: half_block((plane_at * N_AO + along).astype(jnp.int32)), jnp.arange(N_AO, dtype=jnp.int32))
    shifts = (0, 0, 0, -LINE, LINE, -1, 1)

    def contract_block(previous, current, following, plane_at, along):
        block_at = (plane_at * N_AO + along).astype(jnp.int32)
        nearby = lax.dynamic_index_in_dim(table, block_at, 0, keepdims=False)
        sources = (current, previous, following, current, current, current, current)
        total = jnp.zeros((RI, BS, 7 * BS), jnp.float32)
        for which in range(7):
            index_at = jnp.clip(along + shifts[which], 0, N_AO - 1).astype(jnp.int32)
            source_half = lax.dynamic_index_in_dim(sources[which], index_at, 0, keepdims=False)
            pieces = []
            for target_step in stencil_steps:
                target = reach.index(offset_between(target_step, stencil_steps[which], -1))
                pieces.append(source_half[:, :, target * BS:(target + 1) * BS])
            columns = jnp.concatenate(pieces, axis=2)
            occ_row = lax.dynamic_index_in_dim(occ_ext, nearby[which], 0, keepdims=False)
            occ_piece = occ_row[:, reverse_step[which] * BS:(reverse_step[which] + 1) * BS].astype(jnp.float32)
            total = total + jnp.einsum('ml,pms->pls', occ_piece, columns.astype(jnp.float32))
        contracted = total.astype(jnp.bfloat16)
        return lax.dot_general(contracted.reshape(RI, -1), tensor_piece(block_at).reshape(RI, -1), (((1,), (1,)), ((), ())), preferred_element_type=jnp.float32)

    def advance(carry, plane_at):
        previous, current, polar_sum = carry
        following = half_plane(jnp.minimum(plane_at + 1, N_GRP - 1).astype(jnp.int32))
        terms = lax.map(lambda along: contract_block(previous, current, following, plane_at, along), jnp.arange(N_AO, dtype=jnp.int32))
        return ((current, following, polar_sum + lax.optimization_barrier(jnp.sum(terms, axis=0))), None)
    first_plane = half_plane(jnp.int32(0))
    initial = (jnp.zeros_like(first_plane), first_plane, jnp.zeros((RI, RI), jnp.float32))
    finished, ignored = lax.scan(advance, initial, jnp.arange(N_GRP, dtype=jnp.int32))
    return finished[2] / (BS * math.sqrt(NB))
```

```python
import functools
import math

import jax
import jax.numpy as jnp
from jax import lax
from jax.experimental import pallas as pl
from jax.experimental.pallas import tpu as pltpu
from jax.sharding import PartitionSpec as P

MESH = pl.DeviceIdType.MESH
BF16 = jnp.bfloat16
F32 = jnp.float32
STEPS = ((0, 0, 0), (-1, 0, 0), (1, 0, 0), (0, -1, 0), (0, 1, 0), (0, 0, -1), (0, 0, 1))


def second_step(i, j, k):
    want = tuple(STEPS[i][x] + STEPS[j][x] - STEPS[k][x] for x in range(3))
    return STEPS.index(want) if want in STEPS else None


def kernel(
    dims,
    t_ref,
    occ_ref,
    virt_ref,
    tm_ref,
    om_ref,
    vm_ref,
    sz_ref,
    out_ref,
    snd,
    arr,
    tn,
    vn,
    vs,
    xs,
    oexp,
    psend,
    r1,
    r2,
    r3,
    a2a_send,
    a2a_recv,
    ex_send,
    ex_recv,
    v_send,
    v_recv,
    r_send,
    r_recv,
):
    groups, rows, line, slab, bs = dims
    n_ao = rows * line
    width = 7 * bs
    g = lax.axis_index("grp")
    a = lax.axis_index("ao")
    y = a // line
    z = a % line

    def moved(step, sign):
        gg = (g + sign * step[0] + groups) % groups
        yy = (y + sign * step[1] + rows) % rows
        zz = (z + sign * step[2] + line) % line
        return gg, yy * line + zz

    def exists(first, second=(0, 0, 0)):
        gg = g + first[0] + second[0]
        yy = y + first[1] + second[1]
        zz = z + first[2] + second[2]
        inside = (gg >= 0) & (gg < groups) & (yy >= 0) & (yy < rows) & (zz >= 0) & (zz < line)
        return inside.astype(jnp.int32)

    barrier = pltpu.get_barrier_semaphore()

    def greet_ao(d, carry):
        pl.semaphore_signal(
            barrier, inc=1, device_id={"ao": (a + d) % n_ao, "grp": g}, device_id_type=MESH
        )
        return carry

    lax.fori_loop(1, n_ao, greet_ao, 0)

    def greet_grp(d, carry):
        pl.semaphore_signal(
            barrier, inc=1, device_id={"ao": a, "grp": (g + d) % groups}, device_id_type=MESH
        )
        return carry

    lax.fori_loop(1, groups, greet_grp, 0)

    part = n_ao // 2
    n_rows = part * slab
    to = lax.broadcasted_iota(jnp.int32, (n_rows, n_rows), 0)
    frm = lax.broadcasted_iota(jnp.int32, (n_rows, n_rows), 1)
    perm = jnp.where(frm == (to % slab) * part + to // slab, 1.0, 0.0).astype(BF16)
    for half in range(2):
        rows_in = t_ref[:, half * part : (half + 1) * part, :].reshape(n_rows, width)
        moved_rows = jnp.dot(perm, rows_in, preferred_element_type=F32)
        snd[half * part : (half + 1) * part] = moved_rows.reshape(part, slab, width).astype(BF16)

    lane = lax.broadcasted_iota(jnp.int32, (1, width), 1)
    lane_block = lane // bs
    lane_in = lane % bs
    row_at = lax.broadcasted_iota(jnp.int32, (bs, 1), 0)
    size_here = sz_ref[g, a]

    def masked(density, mask_ref):
        bound = jnp.zeros((1, width), jnp.int32)
        for k in range(7):
            gk, ak = moved(STEPS[k], 1)
            value = sz_ref[gk, ak] * mask_ref[k, g, a] * exists(STEPS[k])
            bound = bound + jnp.where(lane_block == k, value, 0)
        keep_col = jnp.where(lane_in < bound, 1.0, 0.0)
        keep_row = jnp.where(row_at < size_here, 1.0, 0.0)
        return (density.astype(F32) * (keep_row * keep_col)).astype(BF16)

    vn[0] = masked(virt_ref[...], vm_ref)

    pl.semaphore_wait(barrier, n_ao - 1 + groups - 1)

    def to_neighbour(ref, k, send, recv):
        gk, ak = moved(STEPS[k], -1)
        return pltpu.make_async_remote_copy(
            src_ref=ref.at[0],
            dst_ref=ref.at[k],
            send_sem=send.at[k - 1],
            recv_sem=recv.at[k - 1],
            device_id={"ao": ak, "grp": gk},
            device_id_type=MESH,
        )

    v_copies = [to_neighbour(vn, k, v_send, v_recv) for k in range(1, 7)]
    for copy in v_copies:
        copy.start()

    def give(d, carry):
        turn = d // rows
        far = line // 2 - (turn + 1) // 2
        z_to = (z + far * (2 * (turn % 2) - 1) + line) % line
        y_to = (y + rows - 1 - d % rows) % rows
        target = y_to * line + z_to
        pltpu.make_async_remote_copy(
            src_ref=snd.at[target],
            dst_ref=arr.at[a],
            send_sem=a2a_send,
            recv_sem=a2a_recv,
            device_id={"ao": target, "grp": g},
            device_id_type=MESH,
        ).start()
        return carry

    lax.fori_loop(0, n_ao - 1, give, 0)
    arr[a] = snd[a]

    occ = masked(occ_ref[...], om_ref)
    spread_rows = jnp.where(
        lax.broadcasted_iota(jnp.int32, (bs * slab, bs), 0) // slab
        == lax.broadcasted_iota(jnp.int32, (bs * slab, bs), 1),
        1.0,
        0.0,
    ).astype(BF16)
    spread_cols = jnp.where(
        lax.broadcasted_iota(jnp.int32, (bs, bs * slab), 1) // slab
        == lax.broadcasted_iota(jnp.int32, (bs, bs * slab), 0),
        1.0,
        0.0,
    ).astype(BF16)
    for i in range(7):
        tall = jnp.dot(spread_rows, occ[:, i * bs : (i + 1) * bs], preferred_element_type=F32)
        oexp[i] = jnp.dot(tall.astype(BF16), spread_cols, preferred_element_type=F32)

    col_on = []
    for i in range(7):
        gi, ai = moved(STEPS[i], 1)
        on = jnp.zeros((1, width), jnp.int32)
        for j in range(7):
            value = tm_ref[j, gi, ai] * exists(STEPS[i], STEPS[j])
            on = on + jnp.where(lane_block == j, value, 0)
        col_on.append(on.astype(F32))
    for k in range(7):
        if k:
            v_copies[k - 1].wait_recv()
        row_on = (tm_ref[k, g, a] * exists(STEPS[k])).astype(F32)
        v_row = vn[k].astype(F32) * row_on
        for i in range(7):
            pieces = []
            for j in range(7):
                k2 = second_step(i, j, k)
                if k2 is None:
                    pieces.append(jnp.zeros((bs, bs), F32))
                else:
                    pieces.append(v_row[:, k2 * bs : (k2 + 1) * bs])
            placed = jnp.concatenate(pieces, axis=1) * col_on[i]
            vs[i, k * bs : (k + 1) * bs, :] = placed.astype(BF16)

    pltpu.make_async_copy(arr.at[pl.ds(0, n_ao - 1)], arr.at[pl.ds(0, n_ao - 1)], a2a_recv).wait()
    tn[0] = arr[...].astype(F32).reshape(bs * slab, width).astype(BF16)
    t_copies = [to_neighbour(tn, k, ex_send, ex_recv) for k in range(1, 7)]
    for copy in t_copies:
        copy.start()

    own = tn[0]
    for i in range(7):
        xs[i] = jnp.dot(own, vs[i], preferred_element_type=F32).astype(BF16)
    total = jnp.zeros((slab, bs * slab), F32)
    for i in range(7):
        if i:
            t_copies[i - 1].wait_recv()
        pairs = lax.dot_general(
            xs[i], tn[i], (((1,), (1,)), ((), ())), preferred_element_type=F32
        )
        weighted = pairs * oexp[i]
        total = total + jnp.sum(weighted.reshape(bs, slab, bs * slab), axis=0)

    part_sum = total[:, 0:128]
    for at in range(1, bs * slab // 128):
        part_sum = part_sum + total[:, at * 128 : (at + 1) * 128]
    shift = 64
    while shift >= slab:
        part_sum = part_sum + pltpu.roll(part_sum, shift, 1)
        shift //= 2

    for p in range(slab):
        psend[p] = part_sum[p : p + 1, :]

    def all_slots(buf, count):
        acc = buf[0]
        for at in range(1, count):
            acc = acc + buf[at]
        return acc

    def wait_bytes(buf, count, sem):
        ref = buf.at[pl.ds(0, count - 1)]
        pltpu.make_async_copy(ref, ref, sem).wait()

    def to_grp(d, carry):
        gg = (g + d) % groups
        pltpu.make_async_remote_copy(
            src_ref=psend.at[gg],
            dst_ref=r1.at[g],
            send_sem=r_send.at[0],
            recv_sem=r_recv.at[0],
            device_id={"ao": a, "grp": gg},
            device_id_type=MESH,
        ).start()
        return carry

    lax.fori_loop(1, groups, to_grp, 0)
    r1[g] = psend[g]
    wait_bytes(r1, groups, r_recv.at[0])
    r2[y] = all_slots(r1, groups)

    def to_rows(d, carry):
        yy = (y + d) % rows
        pltpu.make_async_remote_copy(
            src_ref=r2.at[y],
            dst_ref=r2.at[y],
            send_sem=r_send.at[1],
            recv_sem=r_recv.at[1],
            device_id={"ao": yy * line + z, "grp": g},
            device_id_type=MESH,
        ).start()
        return carry

    lax.fori_loop(1, rows, to_rows, 0)
    wait_bytes(r2, rows, r_recv.at[1])
    r3[z] = all_slots(r2, rows)

    def to_line(d, carry):
        zz = (z + d) % line
        pltpu.make_async_remote_copy(
            src_ref=r3.at[z],
            dst_ref=r3.at[z],
            send_sem=r_send.at[2],
            recv_sem=r_recv.at[2],
            device_id={"ao": y * line + zz, "grp": g},
            device_id_type=MESH,
        ).start()
        return carry

    lax.fori_loop(1, line, to_line, 0)
    wait_bytes(r3, line, r_recv.at[2])
    out_ref[...] = all_slots(r3, line) * (1.0 / (bs * math.sqrt(groups * n_ao)))

    for copy in v_copies + t_copies:
        copy.wait_send()
    wait_bytes(snd, n_ao, a2a_send)
    wait_bytes(r1, groups, r_send.at[0])
    wait_bytes(r2, rows, r_send.at[1])
    wait_bytes(r3, line, r_send.at[2])


def body(three_center, occ_density, virt_density, tensor_mask, occ_mask, virt_mask, block_sizes):
    groups = lax.axis_size("grp")
    n_ao = lax.axis_size("ao")
    rows = 4
    line = n_ao // rows
    slab = three_center.shape[0]
    bs = occ_density.shape[2]
    width = 7 * bs
    dims = (groups, rows, line, slab, bs)
    in_vmem = pl.BlockSpec(memory_space=pltpu.VMEM)
    in_smem = pl.BlockSpec(memory_space=pltpu.SMEM)
    result = pl.pallas_call(
        functools.partial(kernel, dims),
        out_shape=jax.ShapeDtypeStruct((1, 128), F32),
        in_specs=[in_vmem] * 3 + [in_smem] * 4,
        out_specs=in_vmem,
        scratch_shapes=[
            pltpu.VMEM((n_ao, slab, width), BF16),
            pltpu.VMEM((n_ao, slab, width), BF16),
            pltpu.VMEM((7, bs * slab, width), BF16),
            pltpu.VMEM((7, bs, width), BF16),
            pltpu.VMEM((7, width, width), BF16),
            pltpu.VMEM((7, bs * slab, width), BF16),
            pltpu.VMEM((7, bs * slab, bs * slab), F32),
            pltpu.VMEM((slab, 1, 128), F32),
            pltpu.VMEM((groups, 1, 128), F32),
            pltpu.VMEM((rows, 1, 128), F32),
            pltpu.VMEM((line, 1, 128), F32),
            pltpu.SemaphoreType.DMA,
            pltpu.SemaphoreType.DMA,
            pltpu.SemaphoreType.DMA((6,)),
            pltpu.SemaphoreType.DMA((6,)),
            pltpu.SemaphoreType.DMA((6,)),
            pltpu.SemaphoreType.DMA((6,)),
            pltpu.SemaphoreType.DMA((3,)),
            pltpu.SemaphoreType.DMA((3,)),
        ],
        compiler_params=pltpu.CompilerParams(
            collective_id=0, has_side_effects=True, vmem_limit_bytes=48 * 1024 * 1024
        ),
    )(
        three_center,
        occ_density.reshape(bs, width),
        virt_density.reshape(bs, width),
        jnp.transpose(tensor_mask, (2, 0, 1)),
        jnp.transpose(occ_mask, (2, 0, 1)),
        jnp.transpose(virt_mask, (2, 0, 1)),
        block_sizes,
    )
    return result[:, :slab]


def solution(mesh):
    in_specs = (
        P(None, "grp", "ao"),
        P("grp", "ao", None, None),
        P("grp", "ao", None, None),
        P(),
        P(),
        P(),
        P(),
    )
    return jax.shard_map(
        body, mesh=mesh, in_specs=in_specs, out_specs=P("grp", None), check_vma=False
    )
```

```python
import functools
import math

import jax
import jax.numpy as jnp
from jax import lax
from jax.experimental import pallas as pl
from jax.experimental.pallas import tpu as pltpu
from jax.sharding import PartitionSpec as P

MESH = pl.DeviceIdType.MESH
BF16 = jnp.bfloat16
F32 = jnp.float32
STEPS = ((0, 0, 0), (-1, 0, 0), (1, 0, 0), (0, -1, 0), (0, 1, 0), (0, 0, -1), (0, 0, 1))


def second_step(i, j, k):
    want = tuple(STEPS[i][x] + STEPS[j][x] - STEPS[k][x] for x in range(3))
    return STEPS.index(want) if want in STEPS else None


def kernel(
    dims,
    t_hbm,
    occ_hbm,
    virt_hbm,
    tm_hbm,
    om_hbm,
    vm_hbm,
    sz_hbm,
    out_ref,
    t_ref,
    occ_ref,
    virt_ref,
    tm_ref,
    om_ref,
    vm_ref,
    sz_ref,
    load_sem,
    snd,
    arr,
    tn,
    vn,
    vs,
    xs,
    oexp,
    psend,
    r1,
    r3,
    a2a_send,
    a2a_recv,
    ex_send,
    ex_recv,
    v_send,
    v_recv,
    r_send,
    r_recv,
):
    groups, rows, line, slab, bs = dims
    n_ao = rows * line
    width = 7 * bs
    g = lax.axis_index("grp")
    a = lax.axis_index("ao")
    y = a // line
    z = a % line

    def moved(step, sign):
        gg = (g + sign * step[0] + groups) % groups
        yy = (y + sign * step[1] + rows) % rows
        zz = (z + sign * step[2] + line) % line
        return gg, yy * line + zz

    def exists(first, second=(0, 0, 0)):
        gg = g + first[0] + second[0]
        yy = y + first[1] + second[1]
        zz = z + first[2] + second[2]
        inside = (gg >= 0) & (gg < groups) & (yy >= 0) & (yy < rows) & (zz >= 0) & (zz < line)
        return inside.astype(jnp.int32)

    loads = []
    for at, (source, target) in enumerate(
        (
            (virt_hbm, virt_ref),
            (vm_hbm, vm_ref),
            (sz_hbm, sz_ref),
            (t_hbm, t_ref),
            (occ_hbm, occ_ref),
            (om_hbm, om_ref),
            (tm_hbm, tm_ref),
        )
    ):
        loads.append(pltpu.make_async_copy(source, target, load_sem.at[at]))
        loads[-1].start()

    barrier = pltpu.get_barrier_semaphore()

    def greet_ao(d, carry):
        pl.semaphore_signal(
            barrier, inc=1, device_id={"ao": (a + d) % n_ao, "grp": g}, device_id_type=MESH
        )
        return carry

    lax.fori_loop(1, n_ao, greet_ao, 0)

    def greet_sheet(d, carry):
        gg = (g + 1 + d // rows) % groups
        yy = (y + d) % rows
        pl.semaphore_signal(
            barrier, inc=1, device_id={"ao": yy * line + z, "grp": gg}, device_id_type=MESH
        )
        return carry

    lax.fori_loop(0, (groups - 1) * rows, greet_sheet, 0)


    part = n_ao // 2
    loads[3].wait()
    n_rows = part * slab
    to = lax.broadcasted_iota(jnp.int32, (n_rows, n_rows), 0)
    frm = lax.broadcasted_iota(jnp.int32, (n_rows, n_rows), 1)
    perm = jnp.where(frm == (to % slab) * part + to // slab, 1.0, 0.0).astype(BF16)
    for half in range(2):
        rows_in = t_ref[:, half * part : (half + 1) * part, :].reshape(n_rows, width)
        moved_rows = jnp.dot(perm, rows_in, preferred_element_type=F32)
        snd[half * part : (half + 1) * part] = moved_rows.reshape(part, slab, width).astype(BF16)

    lane = lax.broadcasted_iota(jnp.int32, (1, width), 1)
    lane_block = lane // bs
    lane_in = lane % bs
    row_at = lax.broadcasted_iota(jnp.int32, (bs, 1), 0)
    for at in (0, 1, 2):
        loads[at].wait()
    size_here = sz_ref[g, a]

    def masked(density, mask_ref):
        bound = jnp.zeros((1, width), jnp.int32)
        for k in range(7):
            gk, ak = moved(STEPS[k], 1)
            value = sz_ref[gk, ak] * mask_ref[k, g, a] * exists(STEPS[k])
            bound = bound + jnp.where(lane_block == k, value, 0)
        keep_col = jnp.where(lane_in < bound, 1.0, 0.0)
        keep_row = jnp.where(row_at < size_here, 1.0, 0.0)
        return (density.astype(F32) * (keep_row * keep_col)).astype(BF16)

    vn[0] = masked(virt_ref[...], vm_ref)

    pl.semaphore_wait(barrier, n_ao - 1 + (groups - 1) * rows)

    def to_neighbour(ref, k, send, recv):
        gk, ak = moved(STEPS[k], -1)
        return pltpu.make_async_remote_copy(
            src_ref=ref.at[0],
            dst_ref=ref.at[k],
            send_sem=send.at[k - 1],
            recv_sem=recv.at[k - 1],
            device_id={"ao": ak, "grp": gk},
            device_id_type=MESH,
        )

    v_copies = [to_neighbour(vn, k, v_send, v_recv) for k in range(1, 7)]
    for copy in v_copies:
        copy.start()

    def give(d, carry):
        turn = d // rows
        far = line // 2 - (turn + 1) // 2
        z_to = (z + far * (2 * (turn % 2) - 1) + line) % line
        y_to = (y + rows - 1 - d % rows) % rows
        target = y_to * line + z_to
        pltpu.make_async_remote_copy(
            src_ref=snd.at[target],
            dst_ref=arr.at[a],
            send_sem=a2a_send,
            recv_sem=a2a_recv,
            device_id={"ao": target, "grp": g},
            device_id_type=MESH,
        ).start()
        return carry

    lax.fori_loop(0, n_ao - 1, give, 0)
    arr[a] = snd[a]

    for at in (4, 5, 6):
        loads[at].wait()
    occ = masked(occ_ref[...], om_ref)
    spread_rows = jnp.where(
        lax.broadcasted_iota(jnp.int32, (bs * slab, bs), 0) // slab
        == lax.broadcasted_iota(jnp.int32, (bs * slab, bs), 1),
        1.0,
        0.0,
    ).astype(BF16)
    spread_cols = jnp.where(
        lax.broadcasted_iota(jnp.int32, (bs, bs * slab), 1) // slab
        == lax.broadcasted_iota(jnp.int32, (bs, bs * slab), 0),
        1.0,
        0.0,
    ).astype(BF16)
    for i in range(7):
        tall = jnp.dot(spread_rows, occ[:, i * bs : (i + 1) * bs], preferred_element_type=F32)
        oexp[i] = jnp.dot(tall.astype(BF16), spread_cols, preferred_element_type=F32)

    col_on = []
    for i in range(7):
        gi, ai = moved(STEPS[i], 1)
        on = jnp.zeros((1, width), jnp.int32)
        for j in range(7):
            value = tm_ref[j, gi, ai] * exists(STEPS[i], STEPS[j])
            on = on + jnp.where(lane_block == j, value, 0)
        col_on.append(on.astype(F32))
    for k in range(7):
        if k:
            v_copies[k - 1].wait_recv()
        row_on = (tm_ref[k, g, a] * exists(STEPS[k])).astype(F32)
        v_row = vn[k].astype(F32) * row_on
        for i in range(7):
            pieces = []
            for j in range(7):
                k2 = second_step(i, j, k)
                if k2 is None:
                    pieces.append(jnp.zeros((bs, bs), F32))
                else:
                    pieces.append(v_row[:, k2 * bs : (k2 + 1) * bs])
            placed = jnp.concatenate(pieces, axis=1) * col_on[i]
            vs[i, k * bs : (k + 1) * bs, :] = placed.astype(BF16)

    pltpu.make_async_copy(arr.at[pl.ds(0, n_ao - 1)], arr.at[pl.ds(0, n_ao - 1)], a2a_recv).wait()
    tn[0] = arr[...].astype(F32).reshape(bs * slab, width).astype(BF16)
    t_copies = [to_neighbour(tn, k, ex_send, ex_recv) for k in range(1, 7)]
    for copy in t_copies:
        copy.start()

    own = tn[0]
    for i in range(7):
        xs[i] = jnp.dot(own, vs[i], preferred_element_type=F32).astype(BF16)
    total = jnp.zeros((slab, bs * slab), F32)
    for i in range(7):
        if i:
            t_copies[i - 1].wait_recv()
        pairs = lax.dot_general(
            xs[i], tn[i], (((1,), (1,)), ((), ())), preferred_element_type=F32
        )
        weighted = pairs * oexp[i]
        total = total + jnp.sum(weighted.reshape(bs, slab, bs * slab), axis=0)

    part_sum = total[:, 0:128]
    for at in range(1, bs * slab // 128):
        part_sum = part_sum + total[:, at * 128 : (at + 1) * 128]
    shift = 64
    while shift >= slab:
        part_sum = part_sum + pltpu.roll(part_sum, shift, 1)
        shift //= 2

    for p in range(slab):
        psend[p] = part_sum[p : p + 1, :]

    def all_slots(buf, count):
        acc = buf[0]
        for at in range(1, count):
            acc = acc + buf[at]
        return acc

    def wait_bytes(buf, count, sem):
        ref = buf.at[pl.ds(0, count - 1)]
        pltpu.make_async_copy(ref, ref, sem).wait()

    def to_sheet(d, carry):
        gg = (g + d // rows) % groups
        yy = (y + d % rows) % rows
        pltpu.make_async_remote_copy(
            src_ref=psend.at[gg],
            dst_ref=r1.at[g * rows + y],
            send_sem=r_send.at[0],
            recv_sem=r_recv.at[0],
            device_id={"ao": yy * line + z, "grp": gg},
            device_id_type=MESH,
        ).start()
        return carry

    lax.fori_loop(1, groups * rows, to_sheet, 0)
    r1[g * rows + y] = psend[g]
    wait_bytes(r1, groups * rows, r_recv.at[0])
    r3[z] = all_slots(r1, groups * rows)

    def to_line(d, carry):
        zz = (z + d) % line
        pltpu.make_async_remote_copy(
            src_ref=r3.at[z],
            dst_ref=r3.at[z],
            send_sem=r_send.at[1],
            recv_sem=r_recv.at[1],
            device_id={"ao": y * line + zz, "grp": g},
            device_id_type=MESH,
        ).start()
        return carry

    lax.fori_loop(1, line, to_line, 0)
    wait_bytes(r3, line, r_recv.at[1])
    scale = 1.0 / (bs * math.sqrt(groups * n_ao))
    out_ref[...] = (all_slots(r3, line) * scale)[:, :slab]

    for copy in v_copies + t_copies:
        copy.wait_send()
    wait_bytes(snd, n_ao, a2a_send)
    wait_bytes(r1, groups * rows, r_send.at[0])
    wait_bytes(r3, line, r_send.at[1])


def body(three_center, occ_density, virt_density, tensor_mask, occ_mask, virt_mask, block_sizes):
    groups = lax.axis_size("grp")
    n_ao = lax.axis_size("ao")
    rows = 4
    line = n_ao // rows
    slab = three_center.shape[0]
    bs = occ_density.shape[2]
    width = 7 * bs
    dims = (groups, rows, line, slab, bs)
    in_vmem = pl.BlockSpec(memory_space=pltpu.VMEM)
    result = pl.pallas_call(
        functools.partial(kernel, dims),
        out_shape=jax.ShapeDtypeStruct((1, slab), F32),
        in_specs=[pl.BlockSpec(memory_space=pltpu.HBM)] * 7,
        out_specs=in_vmem,
        scratch_shapes=[
            pltpu.VMEM((slab, n_ao, width), BF16),
            pltpu.VMEM((bs, width), BF16),
            pltpu.VMEM((bs, width), BF16),
            pltpu.SMEM((7, groups, n_ao), jnp.int32),
            pltpu.SMEM((7, groups, n_ao), jnp.int32),
            pltpu.SMEM((7, groups, n_ao), jnp.int32),
            pltpu.SMEM((groups, n_ao), jnp.int32),
            pltpu.SemaphoreType.DMA((7,)),
            pltpu.VMEM((n_ao, slab, width), BF16),
            pltpu.VMEM((n_ao, slab, width), BF16),
            pltpu.VMEM((7, bs * slab, width), BF16),
            pltpu.VMEM((7, bs, width), BF16),
            pltpu.VMEM((7, width, width), BF16),
            pltpu.VMEM((7, bs * slab, width), BF16),
            pltpu.VMEM((7, bs * slab, bs * slab), F32),
            pltpu.VMEM((slab, 1, 128), F32),
            pltpu.VMEM((groups * rows, 1, 128), F32),
            pltpu.VMEM((line, 1, 128), F32),
            pltpu.SemaphoreType.DMA,
            pltpu.SemaphoreType.DMA,
            pltpu.SemaphoreType.DMA((6,)),
            pltpu.SemaphoreType.DMA((6,)),
            pltpu.SemaphoreType.DMA((6,)),
            pltpu.SemaphoreType.DMA((6,)),
            pltpu.SemaphoreType.DMA((2,)),
            pltpu.SemaphoreType.DMA((2,)),
        ],
        compiler_params=pltpu.CompilerParams(
            collective_id=0, has_side_effects=True, vmem_limit_bytes=60 * 1024 * 1024
        ),
    )(
        three_center,
        occ_density.reshape(bs, width),
        virt_density.reshape(bs, width),
        jnp.transpose(tensor_mask, (2, 0, 1)),
        jnp.transpose(occ_mask, (2, 0, 1)),
        jnp.transpose(virt_mask, (2, 0, 1)),
        block_sizes,
    )
    return result


def solution(mesh):
    in_specs = (
        P(None, "grp", "ao"),
        P("grp", "ao", None, None),
        P("grp", "ao", None, None),
        P(),
        P(),
        P(),
        P(),
    )
    return jax.shard_map(
        body, mesh=mesh, in_specs=in_specs, out_specs=P("grp", None), check_vma=False
    )
```

```python
import functools
import math

import jax
import jax.numpy as jnp
from jax import lax
from jax.experimental import pallas as pl
from jax.experimental.pallas import tpu as pltpu
from jax.sharding import PartitionSpec as P

MESH = pl.DeviceIdType.MESH
BF16 = jnp.bfloat16
F32 = jnp.float32
STEPS = ((0, 0, 0), (-1, 0, 0), (1, 0, 0), (0, -1, 0), (0, 1, 0), (0, 0, -1), (0, 0, 1))
BACK = (0, 2, 1, 4, 3, 6, 5)
PARTS = 4


def second_step(i, j, k):
    want = tuple(STEPS[i][x] + STEPS[j][x] - STEPS[k][x] for x in range(3))
    return STEPS.index(want) if want in STEPS else None


def kernel(
    dims,
    t_hbm,
    occ_hbm,
    virt_hbm,
    tm_hbm,
    om_hbm,
    vm_hbm,
    sz_hbm,
    out_ref,
    t_ref,
    occ_ref,
    virt_ref,
    tm_ref,
    om_ref,
    vm_ref,
    sz_ref,
    load_sem,
    snd,
    arr,
    tn,
    vn,
    pack,
    vs,
    xs,
    oexp,
    psend,
    r1,
    r3,
    a2a_send,
    a2a_recv,
    ex_send,
    ex_recv,
    v_send,
    v_recv,
    p_send,
    p_recv,
    r_send,
    r_recv,
):
    groups, rows, line, slab, bs = dims
    n_ao = rows * line
    width = 7 * bs
    tall = bs * slab
    g = lax.axis_index("grp")
    a = lax.axis_index("ao")
    y = a // line
    z = a % line
    odd = g % 2
    way = 1 - 2 * odd

    def shifted(dg, dy, dz):
        gg = (g + dg + groups) % groups
        yy = (y + dy + rows) % rows
        zz = (z + dz + line) % line
        return gg, yy * line + zz

    def exists(first, second=(0, 0, 0)):
        gg = g + first[0] + second[0]
        yy = y + first[1] + second[1]
        zz = z + first[2] + second[2]
        inside = (gg >= 0) & (gg < groups) & (yy >= 0) & (yy < rows) & (zz >= 0) & (zz < line)
        return inside.astype(jnp.int32)

    barrier = pltpu.get_barrier_semaphore()

    def far_first(d):
        turn = d // rows
        far = line // 2 - (turn + 1) // 2
        z_to = (z + far * (2 * (turn % 2) - 1) + line) % line
        y_to = (y + rows - 1 - d % rows) % rows
        return y_to * line + z_to

    def greet_ao(d, carry):
        pl.semaphore_signal(
            barrier, inc=1, device_id={"ao": far_first(d), "grp": g}, device_id_type=MESH
        )
        return carry

    lax.fori_loop(0, n_ao - 1, greet_ao, 0)

    def greet_sheet(d, carry):
        gg = (g + 1 + d // rows) % groups
        yy = (y + d) % rows
        pl.semaphore_signal(
            barrier, inc=1, device_id={"ao": yy * line + z, "grp": gg}, device_id_type=MESH
        )
        return carry

    lax.fori_loop(0, (groups - 1) * rows, greet_sheet, 0)

    loads = []
    for at, (source, target) in enumerate(
        (
            (t_hbm, t_ref),
            (virt_hbm, virt_ref),
            (vm_hbm, vm_ref),
            (sz_hbm, sz_ref),
            (occ_hbm, occ_ref),
            (om_hbm, om_ref),
            (tm_hbm, tm_ref),
        )
    ):
        loads.append(pltpu.make_async_copy(source, target, load_sem.at[at]))
        loads[-1].start()

    lane = lax.broadcasted_iota(jnp.int32, (1, width), 1)
    lane_block = lane // bs
    lane_in = lane % bs
    row_at = lax.broadcasted_iota(jnp.int32, (bs, 1), 0)

    def masked(density, mask_ref):
        bound = jnp.zeros((1, width), jnp.int32)
        for k in range(7):
            gk, ak = shifted(*STEPS[k])
            value = sz_ref[gk, ak] * mask_ref[k, g, a] * exists(STEPS[k])
            bound = bound + jnp.where(lane_block == k, value, 0)
        keep_col = jnp.where(lane_in < bound, 1.0, 0.0)
        keep_row = jnp.where(row_at < sz_ref[g, a], 1.0, 0.0)
        return (density.astype(F32) * (keep_row * keep_col)).astype(BF16)

    for at in (1, 2, 3):
        loads[at].wait()
    vn[0] = masked(virt_ref[...], vm_ref)

    loads[0].wait()
    part = n_ao // 2
    n_rows = part * slab
    to = lax.broadcasted_iota(jnp.int32, (n_rows, n_rows), 0)
    frm = lax.broadcasted_iota(jnp.int32, (n_rows, n_rows), 1)
    perm = jnp.where(frm == (to % slab) * part + to // slab, 1.0, 0.0).astype(BF16)
    for half in range(2):
        rows_in = t_ref[:, half * part : (half + 1) * part, :].reshape(n_rows, width)
        moved_rows = jnp.dot(perm, rows_in, preferred_element_type=F32)
        snd[half * part : (half + 1) * part] = moved_rows.reshape(part, slab, width).astype(BF16)

    pl.semaphore_wait(barrier, n_ao - 1 + (groups - 1) * rows)

    def v_copy(k):
        gk, ak = shifted(*(-x for x in STEPS[k]))
        return pltpu.make_async_remote_copy(
            src_ref=vn.at[0],
            dst_ref=vn.at[k],
            send_sem=v_send.at[k - 1],
            recv_sem=v_recv.at[k - 1],
            device_id={"ao": ak, "grp": gk},
            device_id_type=MESH,
        )

    v_copies = [v_copy(k) for k in range(1, 7)]
    for copy in v_copies:
        copy.start()

    def give(d, carry):
        target = far_first(d)
        pltpu.make_async_remote_copy(
            src_ref=snd.at[target],
            dst_ref=arr.at[d],
            send_sem=a2a_send,
            recv_sem=a2a_recv.at[d // (n_ao // PARTS)],
            device_id={"ao": target, "grp": g},
            device_id_type=MESH,
        ).start()
        return carry

    first_sends = n_ao // PARTS
    lax.fori_loop(0, first_sends, give, 0)
    arr[n_ao - 1] = snd[a]

    for at in (4, 5, 6):
        loads[at].wait()
    occ = masked(occ_ref[...], om_ref)

    for copy in v_copies:
        copy.wait_recv()

    def towards(parity, axis):
        return (4 if parity == 0 else 3) if axis == 0 else (6 if parity == 0 else 5)

    def others(step):
        return [k for k in range(1, 7) if k != step]

    def block_of(value, k):
        return value[:, k * bs : (k + 1) * bs]

    for parity in range(2):

        @pl.when(odd == parity)
        def _(parity=parity):
            for axis in range(2):
                step = towards(parity, axis)
                for at, k in enumerate(others(step)):
                    here = block_of(vn[k], BACK[k])
                    there = block_of(occ if k == BACK[step] else vn[k], step)
                    pack[axis, at] = jnp.concatenate([here, there], axis=1)

    def along(axis, sign):
        return shifted(0, sign * way, 0) if axis == 0 else shifted(0, 0, sign * way)

    def p_copy(axis):
        gk, ak = along(axis, 1)
        return pltpu.make_async_remote_copy(
            src_ref=pack.at[axis],
            dst_ref=pack.at[2 + axis],
            send_sem=p_send.at[axis],
            recv_sem=p_recv.at[axis],
            device_id={"ao": ak, "grp": gk},
            device_id_type=MESH,
        )

    p_copies = [p_copy(axis) for axis in range(2)]
    for copy in p_copies:
        copy.start()
    lax.fori_loop(first_sends, n_ao - 1, give, 0)

    def mask_lanes(block_step):
        gi, ai = shifted(*block_step)
        on = jnp.zeros((1, width), jnp.int32)
        for j in range(7):
            value = tm_ref[j, gi, ai] * exists(block_step, STEPS[j])
            on = on + jnp.where(lane_block == j, value, 0)
        return on.astype(F32)

    own_lanes = mask_lanes(STEPS[0])
    nothing = jnp.zeros((bs, bs), F32)

    def place(slot, i, k, row_on, lanes_on, block):
        pieces = []
        for j in range(7):
            k2 = second_step(i, j, k)
            pieces.append(nothing if k2 is None else block(k2).astype(F32))
        placed = jnp.concatenate(pieces, axis=1) * lanes_on * row_on
        vs[slot, k * bs : (k + 1) * bs, :] = placed.astype(BF16)

    def place_all(slot_steps):
        lanes = [mask_lanes(STEPS[i]) for _, i in slot_steps]
        for k in range(7):
            row_on = (tm_ref[k, g, a] * exists(STEPS[k])).astype(F32)
            for (slot, i), lanes_on in zip(slot_steps, lanes):
                place(slot, i, k, row_on, lanes_on, lambda k2: block_of(vn[k], k2))

    place_all([(0, 0), (1, 1), (2, 2)])
    for parity in range(2):

        @pl.when(odd == parity)
        def _(parity=parity):
            place_all([(3, BACK[towards(parity, 0)]), (4, BACK[towards(parity, 1)])])

    def source_of(slot, yy, zz):
        turn = slot >> 2
        far = line // 2 - ((turn + 1) >> 1)
        z_from = (zz - far * (2 * (turn & 1) - 1) + line) & (line - 1)
        return ((yy + 1 + (slot & (rows - 1))) & (rows - 1)) * line + z_from

    def spread(yy, zz):
        down = lax.broadcasted_iota(jnp.int32, (tall, bs), 0) // slab
        across = lax.broadcasted_iota(jnp.int32, (bs, tall), 1) // slab
        tall_at = lax.broadcasted_iota(jnp.int32, (tall, bs), 1)
        wide_at = lax.broadcasted_iota(jnp.int32, (bs, tall), 0)
        as_rows = jnp.where(source_of(down, yy, zz) == tall_at, 1.0, 0.0).astype(BF16)
        as_cols = jnp.where(source_of(across, yy, zz) == wide_at, 1.0, 0.0).astype(BF16)
        return as_rows, as_cols

    own_rows, own_cols = spread(y, z)
    y_rows, y_cols = spread((y - way + rows) % rows, z)
    z_rows, z_cols = spread(y, (z - way + line) % line)

    def weigh(slot, as_rows, block, as_cols):
        stretched = jnp.dot(as_rows, block, preferred_element_type=F32).astype(BF16)
        oexp[slot] = jnp.dot(stretched, as_cols, preferred_element_type=F32)

    def by_way(up, down):
        keep = odd.astype(F32)
        both = block_of(occ, up).astype(F32) * (1.0 - keep) + block_of(occ, down).astype(F32) * keep
        return both.astype(BF16)

    weigh(0, own_rows, block_of(occ, 0), own_cols)
    weigh(1, own_rows, block_of(occ, 1), own_cols)
    weigh(2, own_rows, block_of(occ, 2), own_cols)
    weigh(3, own_rows, by_way(3, 4), y_cols)
    weigh(4, own_rows, by_way(5, 6), z_cols)

    for axis in range(2):
        p_copies[axis].wait_recv()
    for parity in range(2):

        @pl.when(odd == parity)
        def _(parity=parity):
            for axis in range(2):
                i = towards(parity, axis)
                ks = others(i)
                source = STEPS[BACK[i]]
                gs, a_s = shifted(*source)
                for k in range(7):
                    row_on = (tm_ref[k, gs, a_s] * exists(source, STEPS[k])).astype(F32)

                    def block(k2, k=k):
                        if k == 0:
                            return block_of(vn[BACK[i]], k2)
                        if k == i:
                            return block_of(vn[0], k2)
                        half = 0 if k2 == BACK[k] else 1
                        return block_of(pack[2 + axis, ks.index(k)], half)

                    place(5 + axis, i, k, row_on, own_lanes, block)
                received = pack[2 + axis, ks.index(BACK[i])]
                as_rows = y_rows if axis == 0 else z_rows
                weigh(5 + axis, as_rows, block_of(received, 1), own_cols)

    chunk = n_ao // PARTS
    high = chunk * slab

    def t_copy(to, p):
        if to < 2:
            gk, ak = shifted(1 - 2 * to, 0, 0)
        else:
            gk, ak = along(to - 2, 1)
        where = pl.ds(p * high, high)
        return pltpu.make_async_remote_copy(
            src_ref=tn.at[0, where],
            dst_ref=tn.at[1 + to, where],
            send_sem=ex_send.at[to, p],
            recv_sem=ex_recv.at[to, p],
            device_id={"ao": ak, "grp": gk},
            device_id_type=MESH,
        )

    t_copies = [[t_copy(to, p) for p in range(PARTS)] for to in range(4)]
    for p in range(PARTS):
        count = chunk if p < PARTS - 1 else chunk - 1
        arrived = arr.at[pl.ds(p * chunk, count)]
        pltpu.make_async_copy(arrived, arrived, a2a_recv.at[p]).wait()
        here = arr[p * chunk : (p + 1) * chunk].astype(F32).reshape(high, width).astype(BF16)
        tn[0, p * high : (p + 1) * high, :] = here
        for to in (3, 2, 1, 0):
            t_copies[to][p].start()
        for s in range(5):
            xs[s, p * high : (p + 1) * high, :] = jnp.dot(
                here, vs[s], preferred_element_type=F32
            ).astype(BF16)

    def pair_sum(slot, left, right, r0, r1_, c0, c1):
        pairs = lax.dot_general(
            left[r0:r1_], right[c0:c1], (((1,), (1,)), ((), ())), preferred_element_type=F32
        )
        weighted = pairs * oexp[slot, r0:r1_, c0:c1]
        summed = jnp.sum(weighted.reshape((r1_ - r0) // slab, slab, c1 - c0), axis=0)
        folded = summed[:, 0:128]
        for at in range(1, (c1 - c0) // 128):
            folded = folded + summed[:, at * 128 : (at + 1) * 128]
        return folded

    part_sum = pair_sum(0, xs.at[0], tn.at[0], 0, tall, 0, tall)
    early = (PARTS - 1) * high
    for lo, hi, parts in ((0, early, range(PARTS - 1)), (early, tall, (PARTS - 1,))):
        for to in (0, 1, 2, 3):
            for p in parts:
                t_copies[to][p].wait_recv()
            part_sum = part_sum + pair_sum(
                1 + to, xs.at[1 + to], tn.at[1 + to], 0, tall, lo, hi
            )
            if to >= 2:
                s = 3 + to
                xs[s, lo:hi, :] = jnp.dot(
                    tn[1 + to, lo:hi, :], vs[s], preferred_element_type=F32
                ).astype(BF16)
                part_sum = part_sum + pair_sum(s, xs.at[s], tn.at[0], lo, hi, 0, tall)

    shift = 64
    while shift >= slab:
        part_sum = part_sum + pltpu.roll(part_sum, shift, 1)
        shift //= 2

    def wait_bytes(buf, count, sem):
        ref = buf.at[pl.ds(0, count - 1)]
        pltpu.make_async_copy(ref, ref, sem).wait()

    def left_all():
        for copy in v_copies + p_copies + [c for per in t_copies for c in per]:
            copy.wait_send()
        wait_bytes(snd, n_ao, a2a_send)

    for p in range(slab):
        psend[p] = part_sum[p : p + 1, :]

    def all_slots(buf, count):
        acc = buf[0]
        for at in range(1, count):
            acc = acc + buf[at]
        return acc

    def to_sheet(d, carry):
        gg = (g + d // rows) % groups
        yy = (y + d % rows) % rows
        pltpu.make_async_remote_copy(
            src_ref=psend.at[gg],
            dst_ref=r1.at[g * rows + y],
            send_sem=r_send.at[0],
            recv_sem=r_recv.at[0],
            device_id={"ao": yy * line + z, "grp": gg},
            device_id_type=MESH,
        ).start()
        return carry

    lax.fori_loop(1, groups * rows, to_sheet, 0)
    r1[g * rows + y] = psend[g]
    wait_bytes(r1, groups * rows, r_recv.at[0])
    r3[z] = all_slots(r1, groups * rows)

    def to_line(d, carry):
        far = line // 2 - d // 2
        zz = (z + far * (2 * (d % 2) - 1) + line) % line
        pltpu.make_async_remote_copy(
            src_ref=r3.at[z],
            dst_ref=r3.at[z],
            send_sem=r_send.at[1],
            recv_sem=r_recv.at[1],
            device_id={"ao": y * line + zz, "grp": g},
            device_id_type=MESH,
        ).start()
        return carry

    lax.fori_loop(1, line, to_line, 0)
    left_all()
    wait_bytes(r1, groups * rows, r_send.at[0])
    wait_bytes(r3, line, r_recv.at[1])
    scale = 1.0 / (bs * math.sqrt(groups * n_ao))
    out_ref[...] = (all_slots(r3, line) * scale)[:, :slab]
    wait_bytes(r3, line, r_send.at[1])


def body(three_center, occ_density, virt_density, tensor_mask, occ_mask, virt_mask, block_sizes):
    groups = lax.axis_size("grp")
    n_ao = lax.axis_size("ao")
    rows = 4
    line = n_ao // rows
    slab = three_center.shape[0]
    bs = occ_density.shape[2]
    width = 7 * bs
    tall = bs * slab
    dims = (groups, rows, line, slab, bs)
    dma = pltpu.SemaphoreType.DMA
    result = pl.pallas_call(
        functools.partial(kernel, dims),
        out_shape=jax.ShapeDtypeStruct((1, slab), F32),
        in_specs=[pl.BlockSpec(memory_space=pltpu.HBM)] * 7,
        out_specs=pl.BlockSpec(memory_space=pltpu.VMEM),
        scratch_shapes=[
            pltpu.VMEM((slab, n_ao, width), BF16),
            pltpu.VMEM((bs, width), BF16),
            pltpu.VMEM((bs, width), BF16),
            pltpu.SMEM((7, groups, n_ao), jnp.int32),
            pltpu.SMEM((7, groups, n_ao), jnp.int32),
            pltpu.SMEM((7, groups, n_ao), jnp.int32),
            pltpu.SMEM((groups, n_ao), jnp.int32),
            dma((7,)),
            pltpu.VMEM((n_ao, slab, width), BF16),
            pltpu.VMEM((n_ao, slab, width), BF16),
            pltpu.VMEM((5, tall, width), BF16),
            pltpu.VMEM((7, bs, width), BF16),
            pltpu.VMEM((4, 5, bs, 2 * bs), BF16),
            pltpu.VMEM((7, width, width), BF16),
            pltpu.VMEM((7, tall, width), BF16),
            pltpu.VMEM((7, tall, tall), F32),
            pltpu.VMEM((slab, 1, 128), F32),
            pltpu.VMEM((groups * rows, 1, 128), F32),
            pltpu.VMEM((line, 1, 128), F32),
            dma,
            dma((PARTS,)),
            dma((4, PARTS)),
            dma((4, PARTS)),
            dma((6,)),
            dma((6,)),
            dma((2,)),
            dma((2,)),
            dma((2,)),
            dma((2,)),
        ],
        compiler_params=pltpu.CompilerParams(
            collective_id=0, has_side_effects=True, vmem_limit_bytes=60 * 1024 * 1024
        ),
    )(
        three_center,
        occ_density.reshape(bs, width),
        virt_density.reshape(bs, width),
        jnp.transpose(tensor_mask, (2, 0, 1)),
        jnp.transpose(occ_mask, (2, 0, 1)),
        jnp.transpose(virt_mask, (2, 0, 1)),
        block_sizes,
    )
    return result


def solution(mesh):
    in_specs = (
        P(None, "grp", "ao"),
        P("grp", "ao", None, None),
        P("grp", "ao", None, None),
        P(),
        P(),
        P(),
        P(),
    )
    return jax.shard_map(
        body, mesh=mesh, in_specs=in_specs, out_specs=P("grp", None), check_vma=False
    )
```

```python
import functools
import math

import jax
import jax.numpy as jnp
from jax import lax
from jax.experimental import pallas as pl
from jax.experimental.pallas import tpu as pltpu
from jax.sharding import PartitionSpec as P

MESH = pl.DeviceIdType.MESH
BF16 = jnp.bfloat16
F32 = jnp.float32
STEPS = ((0, 0, 0), (-1, 0, 0), (1, 0, 0), (0, -1, 0), (0, 1, 0), (0, 0, -1), (0, 0, 1))
BACK = (0, 2, 1, 4, 3, 6, 5)
PARTS = 4


def second_step(i, j, k):
    want = tuple(STEPS[i][x] + STEPS[j][x] - STEPS[k][x] for x in range(3))
    return STEPS.index(want) if want in STEPS else None


def kernel(
    dims,
    t_hbm,
    occ_hbm,
    virt_hbm,
    tm_hbm,
    om_hbm,
    vm_hbm,
    sz_hbm,
    out_ref,
    t_ref,
    occ_ref,
    virt_ref,
    tm_ref,
    om_ref,
    vm_ref,
    sz_ref,
    load_sem,
    snd,
    arr,
    tn,
    vn,
    pack,
    vs,
    xs,
    oexp,
    psend,
    r1,
    r3,
    y_out,
    y_in,
    z_out,
    tt,
    a2a_send,
    a2a_recv,
    y_send,
    y_recv,
    z_send,
    z_recv,
    ex_send,
    ex_recv,
    v_send,
    v_recv,
    p_send,
    p_recv,
    r_send,
    r_recv,
):
    groups, rows, line, slab, bs = dims
    n_ao = rows * line
    width = 7 * bs
    tall = bs * slab
    main = width // 128 * 128
    g = lax.axis_index("grp")
    a = lax.axis_index("ao")
    y = a // line
    z = a % line
    odd = g % 2
    way = 1 - 2 * odd

    def shifted(dg, dy, dz):
        gg = (g + dg + groups) % groups
        yy = (y + dy + rows) % rows
        zz = (z + dz + line) % line
        return gg, yy * line + zz

    def exists(first, second=(0, 0, 0)):
        gg = g + first[0] + second[0]
        yy = y + first[1] + second[1]
        zz = z + first[2] + second[2]
        inside = (gg >= 0) & (gg < groups) & (yy >= 0) & (yy < rows) & (zz >= 0) & (zz < line)
        return inside.astype(jnp.int32)

    barrier = pltpu.get_barrier_semaphore()

    def far_first(d):
        turn = d // rows
        far = line // 2 - (turn + 1) // 2
        z_to = (z + far * (2 * (turn % 2) - 1) + line) % line
        y_to = (y + rows - 1 - d % rows) % rows
        return y_to * line + z_to

    def greet_ao(d, carry):
        pl.semaphore_signal(
            barrier, inc=1, device_id={"ao": far_first(d), "grp": g}, device_id_type=MESH
        )
        return carry

    lax.fori_loop(0, n_ao - 1, greet_ao, 0)

    def greet_sheet(d, carry):
        gg = (g + 1 + d // rows) % groups
        yy = (y + d) % rows
        pl.semaphore_signal(
            barrier, inc=1, device_id={"ao": yy * line + z, "grp": gg}, device_id_type=MESH
        )
        return carry

    lax.fori_loop(0, (groups - 1) * rows, greet_sheet, 0)

    loads = []
    for at, (source, target) in enumerate(
        (
            (t_hbm, t_ref),
            (virt_hbm, virt_ref),
            (vm_hbm, vm_ref),
            (sz_hbm, sz_ref),
            (occ_hbm, occ_ref),
            (om_hbm, om_ref),
            (tm_hbm, tm_ref),
        )
    ):
        loads.append(pltpu.make_async_copy(source, target, load_sem.at[at]))
        loads[-1].start()

    lane = lax.broadcasted_iota(jnp.int32, (1, width), 1)
    lane_block = lane // bs
    lane_in = lane % bs
    row_at = lax.broadcasted_iota(jnp.int32, (bs, 1), 0)

    def masked(density, mask_ref):
        bound = jnp.zeros((1, width), jnp.int32)
        for k in range(7):
            gk, ak = shifted(*STEPS[k])
            value = sz_ref[gk, ak] * mask_ref[k, g, a] * exists(STEPS[k])
            bound = bound + jnp.where(lane_block == k, value, 0)
        keep_col = jnp.where(lane_in < bound, 1.0, 0.0)
        keep_row = jnp.where(row_at < sz_ref[g, a], 1.0, 0.0)
        return (density.astype(F32) * (keep_row * keep_col)).astype(BF16)

    for at in (1, 2, 3):
        loads[at].wait()
    vn[0] = masked(virt_ref[...], vm_ref)

    loads[0].wait()
    part = n_ao // 2
    n_rows = part * slab
    to = lax.broadcasted_iota(jnp.int32, (n_rows, n_rows), 0)
    frm = lax.broadcasted_iota(jnp.int32, (n_rows, n_rows), 1)
    perm = jnp.where(frm == (to % slab) * part + to // slab, 1.0, 0.0).astype(BF16)
    for half in range(2):
        rows_in = t_ref[:, half * part : (half + 1) * part, :].reshape(n_rows, width)
        moved_rows = jnp.dot(perm, rows_in, preferred_element_type=F32)
        snd[half * part : (half + 1) * part] = (
            moved_rows[:, :main].reshape(part, slab, main).astype(BF16)
        )
        for at in range(rows // 2):
            first = moved_rows[at * 2 * bs : at * 2 * bs + bs, main:]
            second = moved_rows[at * 2 * bs + bs : at * 2 * bs + 2 * bs, main:]
            y_out[half * (rows // 2) + at] = jnp.concatenate([first, second], axis=1).astype(BF16)

    pl.semaphore_wait(barrier, n_ao - 1 + (groups - 1) * rows)

    def v_copy(k):
        gk, ak = shifted(*(-x for x in STEPS[k]))
        return pltpu.make_async_remote_copy(
            src_ref=vn.at[0],
            dst_ref=vn.at[k],
            send_sem=v_send.at[k - 1],
            recv_sem=v_recv.at[k - 1],
            device_id={"ao": ak, "grp": gk},
            device_id_type=MESH,
        )

    v_copies = [v_copy(k) for k in range(1, 7)]
    for copy in v_copies:
        copy.start()

    def give_y(d, carry):
        y_to = (y + d) % rows
        pltpu.make_async_remote_copy(
            src_ref=y_out.at[y_to],
            dst_ref=y_in.at[y],
            send_sem=y_send,
            recv_sem=y_recv,
            device_id={"ao": y_to * line + z, "grp": g},
            device_id_type=MESH,
        ).start()
        return carry

    lax.fori_loop(1, rows, give_y, 0)

    def give(d, carry):
        target = far_first(d)
        pltpu.make_async_remote_copy(
            src_ref=snd.at[target],
            dst_ref=arr.at[d // rows * rows + y],
            send_sem=a2a_send,
            recv_sem=a2a_recv.at[d // (n_ao // PARTS)],
            device_id={"ao": target, "grp": g},
            device_id_type=MESH,
        ).start()
        return carry

    first_sends = n_ao // PARTS
    lax.fori_loop(0, first_sends, give, 0)
    arr[n_ao - rows + y] = snd[a]
    y_in[y] = y_out[y]

    for at in (4, 5, 6):
        loads[at].wait()
    occ = masked(occ_ref[...], om_ref)

    def wait_bytes(buf, count, sem):
        ref = buf.at[pl.ds(0, count - 1)]
        pltpu.make_async_copy(ref, ref, sem).wait()

    wait_bytes(y_in, rows, y_recv)
    for half in range(2):
        pieces = [y_in[at][:, half * bs : (half + 1) * bs].astype(F32) for at in range(rows)]
        upper = jnp.concatenate([pieces[0], pieces[2]], axis=1).reshape(line // 2, slab, 2 * bs)
        lower = jnp.concatenate([pieces[1], pieces[3]], axis=1).reshape(line // 2, slab, 2 * bs)
        z_out[half * (line // 2) : (half + 1) * (line // 2)] = jnp.concatenate(
            [upper, lower], axis=1
        ).astype(BF16)
    deep = 2 * slab

    def give_z(turn, carry):
        far = line // 2 - (turn + 1) // 2
        z_to = (z + far * (2 * (turn % 2) - 1) + line) % line
        pltpu.make_async_remote_copy(
            src_ref=z_out.at[z_to],
            dst_ref=tt.at[0, pl.ds(pl.multiple_of(turn * deep, deep), deep)],
            send_sem=z_send,
            recv_sem=z_recv.at[turn // (line // PARTS)],
            device_id={"ao": y * line + z_to, "grp": g},
            device_id_type=MESH,
        ).start()
        return carry

    lax.fori_loop(0, line - 1, give_z, 0)
    tt[0, (line - 1) * deep : line * deep] = z_out[z]

    for copy in v_copies:
        copy.wait_recv()

    def towards(parity, axis):
        return (4 if parity == 0 else 3) if axis == 0 else (6 if parity == 0 else 5)

    def others(step):
        return [k for k in range(1, 7) if k != step]

    def block_of(value, k):
        return value[:, k * bs : (k + 1) * bs]

    for parity in range(2):

        @pl.when(odd == parity)
        def _(parity=parity):
            for axis in range(2):
                step = towards(parity, axis)
                for at, k in enumerate(others(step)):
                    here = block_of(vn[k], BACK[k])
                    there = block_of(occ if k == BACK[step] else vn[k], step)
                    pack[axis, at] = jnp.concatenate([here, there], axis=1)

    def along(axis, sign):
        return shifted(0, sign * way, 0) if axis == 0 else shifted(0, 0, sign * way)

    def p_copy(axis):
        gk, ak = along(axis, 1)
        return pltpu.make_async_remote_copy(
            src_ref=pack.at[axis],
            dst_ref=pack.at[2 + axis],
            send_sem=p_send.at[axis],
            recv_sem=p_recv.at[axis],
            device_id={"ao": ak, "grp": gk},
            device_id_type=MESH,
        )

    p_copies = [p_copy(axis) for axis in range(2)]
    for copy in p_copies:
        copy.start()
    lax.fori_loop(first_sends, n_ao - 1, give, 0)

    def mask_lanes(block_step):
        gi, ai = shifted(*block_step)
        on = jnp.zeros((1, width), jnp.int32)
        for j in range(7):
            value = tm_ref[j, gi, ai] * exists(block_step, STEPS[j])
            on = on + jnp.where(lane_block == j, value, 0)
        return on.astype(F32)

    own_lanes = mask_lanes(STEPS[0])
    nothing = jnp.zeros((bs, bs), F32)

    def place(slot, i, k, row_on, lanes_on, block):
        pieces = []
        for j in range(7):
            k2 = second_step(i, j, k)
            pieces.append(nothing if k2 is None else block(k2).astype(F32))
        placed = jnp.concatenate(pieces, axis=1) * lanes_on * row_on
        vs[slot, k * bs : (k + 1) * bs, :] = placed.astype(BF16)

    def place_all(slot_steps):
        lanes = [mask_lanes(STEPS[i]) for _, i in slot_steps]
        for k in range(7):
            row_on = (tm_ref[k, g, a] * exists(STEPS[k])).astype(F32)
            for (slot, i), lanes_on in zip(slot_steps, lanes):
                place(slot, i, k, row_on, lanes_on, lambda k2: block_of(vn[k], k2))

    place_all([(0, 0), (1, 1), (2, 2)])
    for parity in range(2):

        @pl.when(odd == parity)
        def _(parity=parity):
            place_all([(3, BACK[towards(parity, 0)]), (4, BACK[towards(parity, 1)])])

    def source_of(slot, zz):
        turn = slot >> 2
        far = line // 2 - ((turn + 1) >> 1)
        z_from = (zz - far * (2 * (turn & 1) - 1) + line) & (line - 1)
        return (slot & (rows - 1)) * line + z_from

    def spread(zz):
        down = lax.broadcasted_iota(jnp.int32, (tall, bs), 0) // slab
        across = lax.broadcasted_iota(jnp.int32, (bs, tall), 1) // slab
        tall_at = lax.broadcasted_iota(jnp.int32, (tall, bs), 1)
        wide_at = lax.broadcasted_iota(jnp.int32, (bs, tall), 0)
        as_rows = jnp.where(source_of(down, zz) == tall_at, 1.0, 0.0).astype(BF16)
        as_cols = jnp.where(source_of(across, zz) == wide_at, 1.0, 0.0).astype(BF16)
        return as_rows, as_cols

    own_rows, own_cols = spread(z)
    z_rows, z_cols = spread((z - way + line) % line)

    def weigh(slot, as_rows, block, as_cols):
        stretched = jnp.dot(as_rows, block, preferred_element_type=F32).astype(BF16)
        oexp[slot] = jnp.dot(stretched, as_cols, preferred_element_type=F32)

    def by_way(up, down):
        keep = odd.astype(F32)
        both = block_of(occ, up).astype(F32) * (1.0 - keep) + block_of(occ, down).astype(F32) * keep
        return both.astype(BF16)

    weigh(0, own_rows, block_of(occ, 0), own_cols)
    weigh(1, own_rows, block_of(occ, 1), own_cols)
    weigh(2, own_rows, block_of(occ, 2), own_cols)
    weigh(3, own_rows, by_way(3, 4), own_cols)
    weigh(4, own_rows, by_way(5, 6), z_cols)

    for axis in range(2):
        p_copies[axis].wait_recv()
    for parity in range(2):

        @pl.when(odd == parity)
        def _(parity=parity):
            for axis in range(2):
                i = towards(parity, axis)
                ks = others(i)
                source = STEPS[BACK[i]]
                gs, a_s = shifted(*source)
                for k in range(7):
                    row_on = (tm_ref[k, gs, a_s] * exists(source, STEPS[k])).astype(F32)

                    def block(k2, k=k):
                        if k == 0:
                            return block_of(vn[BACK[i]], k2)
                        if k == i:
                            return block_of(vn[0], k2)
                        half = 0 if k2 == BACK[k] else 1
                        return block_of(pack[2 + axis, ks.index(k)], half)

                    place(5 + axis, i, k, row_on, own_lanes, block)
                received = pack[2 + axis, ks.index(BACK[i])]
                as_rows = own_rows if axis == 0 else z_rows
                weigh(5 + axis, as_rows, block_of(received, 1), own_cols)

    chunk = n_ao // PARTS
    high = chunk * slab

    def t_copy(to, p, lanes):
        if to < 2:
            gk, ak = shifted(1 - 2 * to, 0, 0)
        else:
            gk, ak = along(to - 2, 1)
        if lanes:
            here = tn.at[0, pl.ds(p * high, high), pl.ds(0, main)]
            there = tn.at[1 + to, pl.ds(p * high, high), pl.ds(0, main)]
        else:
            here = tt.at[0, pl.ds(p * high // 2, high // 2)]
            there = tt.at[1 + to, pl.ds(p * high // 2, high // 2)]
        return pltpu.make_async_remote_copy(
            src_ref=here,
            dst_ref=there,
            send_sem=ex_send.at[to, p, lanes],
            recv_sem=ex_recv.at[to, p, lanes],
            device_id={"ao": ak, "grp": gk},
            device_id_type=MESH,
        )

    t_copies = [[[t_copy(to, p, lanes) for lanes in range(2)] for p in range(PARTS)] for to in range(4)]

    def unpack_tail(at, p):
        last = tt[at, p * high // 2 : (p + 1) * high // 2, :].astype(F32)
        last = last.reshape(line // PARTS, deep, 2 * bs)
        both = jnp.concatenate([last[:, :, :bs], last[:, :, bs:]], axis=1)
        tn[at, p * high : (p + 1) * high, main:] = both.reshape(high, bs).astype(BF16)

    for p in range(PARTS):
        count = chunk if p < PARTS - 1 else chunk - 1
        arrived = arr.at[pl.ds(p * chunk, count)]
        pltpu.make_async_copy(arrived, arrived, a2a_recv.at[p]).wait()
        tn[0, p * high : (p + 1) * high, :main] = (
            arr[p * chunk : (p + 1) * chunk].astype(F32).reshape(high, main).astype(BF16)
        )
        for to in (3, 2, 1, 0):
            t_copies[to][p][1].start()
        turns = line // PARTS if p < PARTS - 1 else line // PARTS - 1
        arrived = tt.at[0, pl.ds(p * high // 2, turns * deep)]
        pltpu.make_async_copy(arrived, arrived, z_recv.at[p]).wait()
        for to in (3, 2, 1, 0):
            t_copies[to][p][0].start()
        unpack_tail(0, p)
        here = tn[0, p * high : (p + 1) * high, :]
        for s in range(5):
            xs[s, p * high : (p + 1) * high, :] = jnp.dot(
                here, vs[s], preferred_element_type=F32
            ).astype(BF16)

    def pair_sum(slot, left, right, r0, r1_, c0, c1):
        pairs = lax.dot_general(
            left[r0:r1_], right[c0:c1], (((1,), (1,)), ((), ())), preferred_element_type=F32
        )
        weighted = pairs * oexp[slot, r0:r1_, c0:c1]
        summed = jnp.sum(weighted.reshape((r1_ - r0) // slab, slab, c1 - c0), axis=0)
        folded = summed[:, 0:128]
        for at in range(1, (c1 - c0) // 128):
            folded = folded + summed[:, at * 128 : (at + 1) * 128]
        return folded

    part_sum = pair_sum(0, xs.at[0], tn.at[0], 0, tall, 0, tall)
    early = (PARTS - 1) * high
    for lo, hi, parts in ((0, early, range(PARTS - 1)), (early, tall, (PARTS - 1,))):
        for to in (0, 1, 2, 3):
            for p in parts:
                for copy in t_copies[to][p]:
                    copy.wait_recv()
                unpack_tail(1 + to, p)
            part_sum = part_sum + pair_sum(
                1 + to, xs.at[1 + to], tn.at[1 + to], 0, tall, lo, hi
            )
            if to >= 2:
                s = 3 + to
                xs[s, lo:hi, :] = jnp.dot(
                    tn[1 + to, lo:hi, :], vs[s], preferred_element_type=F32
                ).astype(BF16)
                part_sum = part_sum + pair_sum(s, xs.at[s], tn.at[0], lo, hi, 0, tall)

    shift = 64
    while shift >= slab:
        part_sum = part_sum + pltpu.roll(part_sum, shift, 1)
        shift //= 2

    def left_all():
        for copy in v_copies + p_copies + [c for per in t_copies for two in per for c in two]:
            copy.wait_send()
        wait_bytes(snd, n_ao, a2a_send)
        wait_bytes(y_out, rows, y_send)
        wait_bytes(z_out, line, z_send)

    for p in range(slab):
        psend[p] = part_sum[p : p + 1, :]

    def all_slots(buf, count):
        acc = buf[0]
        for at in range(1, count):
            acc = acc + buf[at]
        return acc

    def to_sheet(d, carry):
        gg = (g + d // rows) % groups
        yy = (y + d % rows) % rows
        pltpu.make_async_remote_copy(
            src_ref=psend.at[gg],
            dst_ref=r1.at[g * rows + y],
            send_sem=r_send.at[0],
            recv_sem=r_recv.at[0],
            device_id={"ao": yy * line + z, "grp": gg},
            device_id_type=MESH,
        ).start()
        return carry

    lax.fori_loop(1, groups * rows, to_sheet, 0)
    r1[g * rows + y] = psend[g]
    wait_bytes(r1, groups * rows, r_recv.at[0])
    r3[z] = all_slots(r1, groups * rows)

    def to_line(d, carry):
        far = line // 2 - d // 2
        zz = (z + far * (2 * (d % 2) - 1) + line) % line
        pltpu.make_async_remote_copy(
            src_ref=r3.at[z],
            dst_ref=r3.at[z],
            send_sem=r_send.at[1],
            recv_sem=r_recv.at[1],
            device_id={"ao": y * line + zz, "grp": g},
            device_id_type=MESH,
        ).start()
        return carry

    lax.fori_loop(1, line, to_line, 0)
    left_all()
    wait_bytes(r1, groups * rows, r_send.at[0])
    wait_bytes(r3, line, r_recv.at[1])
    scale = 1.0 / (bs * math.sqrt(groups * n_ao))
    out_ref[...] = (all_slots(r3, line) * scale)[:, :slab]
    wait_bytes(r3, line, r_send.at[1])


def body(three_center, occ_density, virt_density, tensor_mask, occ_mask, virt_mask, block_sizes):
    groups = lax.axis_size("grp")
    n_ao = lax.axis_size("ao")
    rows = 4
    line = n_ao // rows
    slab = three_center.shape[0]
    bs = occ_density.shape[2]
    width = 7 * bs
    tall = bs * slab
    dims = (groups, rows, line, slab, bs)
    dma = pltpu.SemaphoreType.DMA
    result = pl.pallas_call(
        functools.partial(kernel, dims),
        out_shape=jax.ShapeDtypeStruct((1, slab), F32),
        in_specs=[pl.BlockSpec(memory_space=pltpu.HBM)] * 7,
        out_specs=pl.BlockSpec(memory_space=pltpu.VMEM),
        scratch_shapes=[
            pltpu.VMEM((slab, n_ao, width), BF16),
            pltpu.VMEM((bs, width), BF16),
            pltpu.VMEM((bs, width), BF16),
            pltpu.SMEM((7, groups, n_ao), jnp.int32),
            pltpu.SMEM((7, groups, n_ao), jnp.int32),
            pltpu.SMEM((7, groups, n_ao), jnp.int32),
            pltpu.SMEM((groups, n_ao), jnp.int32),
            dma((7,)),
            pltpu.VMEM((n_ao, slab, width // 128 * 128), BF16),
            pltpu.VMEM((n_ao, slab, width // 128 * 128), BF16),
            pltpu.VMEM((5, tall, width), BF16),
            pltpu.VMEM((7, bs, width), BF16),
            pltpu.VMEM((4, 5, bs, 2 * bs), BF16),
            pltpu.VMEM((7, width, width), BF16),
            pltpu.VMEM((7, tall, width), BF16),
            pltpu.VMEM((7, tall, tall), F32),
            pltpu.VMEM((slab, 1, 128), F32),
            pltpu.VMEM((groups * rows, 1, 128), F32),
            pltpu.VMEM((line, 1, 128), F32),
            pltpu.VMEM((rows, bs, 2 * bs), BF16),
            pltpu.VMEM((rows, bs, 2 * bs), BF16),
            pltpu.VMEM((line, 2 * slab, 2 * bs), BF16),
            pltpu.VMEM((5, line * 2 * slab, 2 * bs), BF16),
            dma,
            dma((PARTS,)),
            dma,
            dma,
            dma,
            dma((PARTS,)),
            dma((4, PARTS, 2)),
            dma((4, PARTS, 2)),
            dma((6,)),
            dma((6,)),
            dma((2,)),
            dma((2,)),
            dma((2,)),
            dma((2,)),
        ],
        compiler_params=pltpu.CompilerParams(
            collective_id=0, has_side_effects=True, vmem_limit_bytes=60 * 1024 * 1024
        ),
    )(
        three_center,
        occ_density.reshape(bs, width),
        virt_density.reshape(bs, width),
        jnp.transpose(tensor_mask, (2, 0, 1)),
        jnp.transpose(occ_mask, (2, 0, 1)),
        jnp.transpose(virt_mask, (2, 0, 1)),
        block_sizes,
    )
    return result


def solution(mesh):
    in_specs = (
        P(None, "grp", "ao"),
        P("grp", "ao", None, None),
        P("grp", "ao", None, None),
        P(),
        P(),
        P(),
        P(),
    )
    return jax.shard_map(
        body, mesh=mesh, in_specs=in_specs, out_specs=P("grp", None), check_vma=False
    )
```

```python
import functools
import math

import jax
import jax.numpy as jnp
from jax import lax
from jax.experimental import pallas as pl
from jax.experimental.pallas import tpu as pltpu
from jax.sharding import PartitionSpec as P

MESH = pl.DeviceIdType.MESH
BF16 = jnp.bfloat16
F32 = jnp.float32
STEPS = ((0, 0, 0), (-1, 0, 0), (1, 0, 0), (0, -1, 0), (0, 1, 0), (0, 0, -1), (0, 0, 1))
BACK = (0, 2, 1, 4, 3, 6, 5)
PARTS = 4


def second_step(i, j, k):
    want = tuple(STEPS[i][x] + STEPS[j][x] - STEPS[k][x] for x in range(3))
    return STEPS.index(want) if want in STEPS else None


def kernel(
    dims,
    t_hbm,
    occ_hbm,
    virt_hbm,
    tm_hbm,
    om_hbm,
    vm_hbm,
    sz_hbm,
    out_ref,
    t_ref,
    occ_ref,
    virt_ref,
    tm_ref,
    om_ref,
    vm_ref,
    sz_ref,
    load_sem,
    snd,
    arr,
    tn,
    vn,
    pack,
    vs,
    xs,
    oexp,
    psend,
    r1,
    r3,
    y_out,
    y_in,
    z_out,
    tt,
    a2a_send,
    a2a_recv,
    y_send,
    y_recv,
    z_send,
    z_recv,
    ex_send,
    ex_recv,
    v_send,
    v_recv,
    p_send,
    p_recv,
    r_send,
    r_recv,
):
    groups, rows, line, slab, bs = dims
    n_ao = rows * line
    width = 7 * bs
    tall = bs * slab
    main = width // 128 * 128
    g = lax.axis_index("grp")
    a = lax.axis_index("ao")
    y = a // line
    z = a % line
    odd = g % 2
    way = 1 - 2 * odd

    def shifted(dg, dy, dz):
        gg = (g + dg + groups) % groups
        yy = (y + dy + rows) % rows
        zz = (z + dz + line) % line
        return gg, yy * line + zz

    def exists(first, second=(0, 0, 0)):
        gg = g + first[0] + second[0]
        yy = y + first[1] + second[1]
        zz = z + first[2] + second[2]
        inside = (gg >= 0) & (gg < groups) & (yy >= 0) & (yy < rows) & (zz >= 0) & (zz < line)
        return inside.astype(jnp.int32)

    loads = []
    for at, (source, target) in enumerate(
        (
            (t_hbm, t_ref),
            (virt_hbm, virt_ref),
            (vm_hbm, vm_ref),
            (sz_hbm, sz_ref),
            (occ_hbm, occ_ref),
            (om_hbm, om_ref),
            (tm_hbm, tm_ref),
        )
    ):
        loads.append(pltpu.make_async_copy(source, target, load_sem.at[at]))
        loads[-1].start()

    barrier = pltpu.get_barrier_semaphore()
    half_line = line // 2
    y_at = [lax.rem(y + rows - 1 - q, rows) for q in range(rows)]
    across_line = lax.rem(z + half_line, line)

    def both_ways(i):
        far = half_line - i
        return (
            (lax.rem(z + far, line), 2 * i - 1),
            (lax.rem(z - far + line, line), 2 * i),
        )

    def greet(aa, gg):
        pl.semaphore_signal(barrier, inc=1, device_id={"ao": aa, "grp": gg}, device_id_type=MESH)

    for q in range(rows):
        greet(y_at[q] * line + across_line, g)

    def greet_ao(i, carry):
        for z_to, _ in both_ways(i):
            for q in range(rows):
                greet(y_at[q] * line + z_to, g)
        return carry

    lax.fori_loop(1, half_line, greet_ao, 0)
    for q in range(rows - 1):
        greet(y_at[q] * line + z, g)

    def greet_sheet(d, carry):
        gg = lax.rem(g + d, groups)
        for q in range(rows):
            greet(y_at[q] * line + z, gg)
        return carry

    lax.fori_loop(1, groups, greet_sheet, 0)

    lane = lax.broadcasted_iota(jnp.int32, (1, width), 1)
    lane_block = lane // bs
    lane_in = lane % bs
    row_at = lax.broadcasted_iota(jnp.int32, (bs, 1), 0)

    def masked(density, mask_ref):
        bound = jnp.zeros((1, width), jnp.int32)
        for k in range(7):
            gk, ak = shifted(*STEPS[k])
            value = sz_ref[gk, ak] * mask_ref[k, g, a] * exists(STEPS[k])
            bound = bound + jnp.where(lane_block == k, value, 0)
        keep_col = jnp.where(lane_in < bound, 1.0, 0.0)
        keep_row = jnp.where(row_at < sz_ref[g, a], 1.0, 0.0)
        return (density.astype(F32) * (keep_row * keep_col)).astype(BF16)

    for at in (1, 2, 3):
        loads[at].wait()
    vn[0] = masked(virt_ref[...], vm_ref)

    loads[0].wait()
    part = n_ao // 2
    n_rows = part * slab
    to = lax.broadcasted_iota(jnp.int32, (n_rows, n_rows), 0)
    frm = lax.broadcasted_iota(jnp.int32, (n_rows, n_rows), 1)
    perm = jnp.where(frm == (to % slab) * part + to // slab, 1.0, 0.0).astype(BF16)
    for half in range(2):
        rows_in = t_ref[:, half * part : (half + 1) * part, :].reshape(n_rows, width)
        moved_rows = jnp.dot(perm, rows_in, preferred_element_type=F32)
        snd[half * part : (half + 1) * part] = (
            moved_rows[:, :main].reshape(part, slab, main).astype(BF16)
        )
        for at in range(rows // 2):
            first = moved_rows[at * 2 * bs : at * 2 * bs + bs, main:]
            second = moved_rows[at * 2 * bs + bs : at * 2 * bs + 2 * bs, main:]
            y_out[half * (rows // 2) + at] = jnp.concatenate([first, second], axis=1).astype(BF16)

    pl.semaphore_wait(barrier, n_ao - 1 + (groups - 1) * rows)

    def v_copy(k):
        gk, ak = shifted(*(-x for x in STEPS[k]))
        return pltpu.make_async_remote_copy(
            src_ref=vn.at[0],
            dst_ref=vn.at[k],
            send_sem=v_send.at[k - 1],
            recv_sem=v_recv.at[k - 1],
            device_id={"ao": ak, "grp": gk},
            device_id_type=MESH,
        )

    def give_y(q):
        return pltpu.make_async_remote_copy(
            src_ref=y_out.at[y_at[q]],
            dst_ref=y_in.at[y],
            send_sem=y_send,
            recv_sem=y_recv,
            device_id={"ao": y_at[q] * line + z, "grp": g},
            device_id_type=MESH,
        )

    for q in range(rows - 1):
        give_y(q).start()

    def place_at(steps):
        return lax.rem(z + way * steps + line, line)

    def give(turn, z_to, z_block, count=rows):
        for q in range(count):
            pltpu.make_async_remote_copy(
                src_ref=snd.at[y_at[q] * line + z_block],
                dst_ref=arr.at[turn * rows + y],
                send_sem=a2a_send,
                recv_sem=a2a_recv.at[turn // (line // PARTS)],
                device_id={"ao": y_at[q] * line + z_to, "grp": g},
                device_id_type=MESH,
            ).start()

    def give_ahead(turn, carry):
        far = half_line - 1 - turn
        give(turn, place_at(-far), place_at(-far - 1))
        return carry

    def give_own(turn, carry):
        z_to = place_at(line - 1 - turn)
        give(turn, z_to, z_to)
        return carry

    give_ahead(0, 0)
    give_ahead(1, 0)
    v_copies = [v_copy(k) for k in range(1, 7)]
    for copy in v_copies:
        copy.start()
    arr[(half_line - 1) * rows + y] = snd[y * line + place_at(-1)]
    arr[n_ao - rows + y] = snd[a]
    y_in[y] = y_out[y]

    for at in (4, 5, 6):
        loads[at].wait()
    occ = masked(occ_ref[...], om_ref)

    def wait_bytes(buf, count, sem):
        ref = buf.at[pl.ds(0, count - 1)]
        pltpu.make_async_copy(ref, ref, sem).wait()

    wait_bytes(y_in, rows, y_recv)
    for half in range(2):
        pieces = [y_in[at][:, half * bs : (half + 1) * bs].astype(F32) for at in range(rows)]
        upper = jnp.concatenate([pieces[0], pieces[2]], axis=1).reshape(line // 2, slab, 2 * bs)
        lower = jnp.concatenate([pieces[1], pieces[3]], axis=1).reshape(line // 2, slab, 2 * bs)
        z_out[half * (line // 2) : (half + 1) * (line // 2)] = jnp.concatenate(
            [upper, lower], axis=1
        ).astype(BF16)
    deep = 2 * slab

    def give_z(slot, turn, z_to, z_block):
        pltpu.make_async_remote_copy(
            src_ref=z_out.at[z_block],
            dst_ref=tt.at[slot, pl.ds(pl.multiple_of(turn * deep, deep), deep)],
            send_sem=z_send,
            recv_sem=z_recv.at[turn // (line // PARTS)],
            device_id={"ao": y * line + z_to, "grp": g},
            device_id_type=MESH,
        ).start()

    def give_z_ahead(turn, carry):
        far = half_line - 1 - turn
        give_z(4, turn, place_at(-far), place_at(-far - 1))
        return carry

    def give_z_own(turn, carry):
        z_to = place_at(line - 1 - turn)
        give_z(0, turn, z_to, z_to)
        return carry

    lax.fori_loop(0, half_line - 1, give_z_ahead, 0)
    lax.fori_loop(half_line, line - 1, give_z_own, 0)
    tt[4, (half_line - 1) * deep : half_line * deep] = z_out[place_at(-1)]
    tt[0, (line - 1) * deep : line * deep] = z_out[z]

    for copy in v_copies:
        copy.wait_recv()

    def towards(parity, axis):
        return (4 if parity == 0 else 3) if axis == 0 else (6 if parity == 0 else 5)

    def others(step):
        return [k for k in range(1, 7) if k != step]

    def block_of(value, k):
        return value[:, k * bs : (k + 1) * bs]

    for parity in range(2):

        @pl.when(odd == parity)
        def _(parity=parity):
            for axis in range(2):
                step = towards(parity, axis)
                for at, k in enumerate(others(step)):
                    here = block_of(vn[k], BACK[k])
                    there = block_of(occ if k == BACK[step] else vn[k], step)
                    pack[axis, at] = jnp.concatenate([here, there], axis=1)

    def along(axis, sign):
        return shifted(0, sign * way, 0) if axis == 0 else shifted(0, 0, sign * way)

    def p_copy(axis):
        gk, ak = along(axis, 1)
        return pltpu.make_async_remote_copy(
            src_ref=pack.at[axis],
            dst_ref=pack.at[2 + axis],
            send_sem=p_send.at[axis],
            recv_sem=p_recv.at[axis],
            device_id={"ao": ak, "grp": gk},
            device_id_type=MESH,
        )

    p_copies = [p_copy(axis) for axis in range(2)]
    for copy in p_copies:
        copy.start()
    lax.fori_loop(2, half_line - 1, give_ahead, 0)
    give(half_line - 1, z, place_at(-1), rows - 1)
    lax.fori_loop(half_line, line - 1, give_own, 0)
    give(line - 1, z, z, rows - 1)

    def mask_lanes(block_step):
        gi, ai = shifted(*block_step)
        on = jnp.zeros((1, width), jnp.int32)
        for j in range(7):
            value = tm_ref[j, gi, ai] * exists(block_step, STEPS[j])
            on = on + jnp.where(lane_block == j, value, 0)
        return on.astype(F32)

    own_lanes = mask_lanes(STEPS[0])
    nothing = jnp.zeros((bs, bs), F32)

    def place(slot, i, k, row_on, lanes_on, block):
        pieces = []
        for j in range(7):
            k2 = second_step(i, j, k)
            pieces.append(nothing if k2 is None else block(k2).astype(F32))
        placed = jnp.concatenate(pieces, axis=1) * lanes_on * row_on
        vs[slot, k * bs : (k + 1) * bs, :] = placed.astype(BF16)

    def place_all(slot_steps):
        lanes = [mask_lanes(STEPS[i]) for _, i in slot_steps]
        for k in range(7):
            row_on = (tm_ref[k, g, a] * exists(STEPS[k])).astype(F32)
            for (slot, i), lanes_on in zip(slot_steps, lanes):
                place(slot, i, k, row_on, lanes_on, lambda k2: block_of(vn[k], k2))

    place_all([(0, 0), (1, 1), (2, 2)])
    for parity in range(2):

        @pl.when(odd == parity)
        def _(parity=parity):
            place_all([(3, BACK[towards(parity, 0)]), (4, BACK[towards(parity, 1)])])

    def source_of(slot, zz, ww):
        turn = slot >> 2
        ahead = jnp.where(turn < half_line, half_line - turn, turn - (line - 1))
        return (slot & (rows - 1)) * line + ((zz + ww * ahead + line) & (line - 1))

    def spread(zz, ww):
        down = lax.broadcasted_iota(jnp.int32, (tall, bs), 0) // slab
        across = lax.broadcasted_iota(jnp.int32, (bs, tall), 1) // slab
        tall_at = lax.broadcasted_iota(jnp.int32, (tall, bs), 1)
        wide_at = lax.broadcasted_iota(jnp.int32, (bs, tall), 0)
        as_rows = jnp.where(source_of(down, zz, ww) == tall_at, 1.0, 0.0).astype(BF16)
        as_cols = jnp.where(source_of(across, zz, ww) == wide_at, 1.0, 0.0).astype(BF16)
        return as_rows, as_cols

    own_rows, own_cols = spread(z, way)
    x_cols = spread(z, -way)[1]
    z_rows, z_cols = spread(place_at(-1), way)

    def weigh(slot, as_rows, block, as_cols):
        stretched = jnp.dot(as_rows, block, preferred_element_type=F32).astype(BF16)
        oexp[slot] = jnp.dot(stretched, as_cols, preferred_element_type=F32)

    def by_way(up, down):
        keep = odd.astype(F32)
        both = block_of(occ, up).astype(F32) * (1.0 - keep) + block_of(occ, down).astype(F32) * keep
        return both.astype(BF16)

    weigh(0, own_rows, block_of(occ, 0), own_cols)
    weigh(1, own_rows, block_of(occ, 1), x_cols)
    weigh(2, own_rows, block_of(occ, 2), x_cols)
    weigh(3, own_rows, by_way(3, 4), own_cols)
    weigh(4, own_rows, by_way(5, 6), z_cols)

    for axis in range(2):
        p_copies[axis].wait_recv()
    for parity in range(2):

        @pl.when(odd == parity)
        def _(parity=parity):
            for axis in range(2):
                i = towards(parity, axis)
                ks = others(i)
                source = STEPS[BACK[i]]
                gs, a_s = shifted(*source)
                for k in range(7):
                    row_on = (tm_ref[k, gs, a_s] * exists(source, STEPS[k])).astype(F32)

                    def block(k2, k=k):
                        if k == 0:
                            return block_of(vn[BACK[i]], k2)
                        if k == i:
                            return block_of(vn[0], k2)
                        half = 0 if k2 == BACK[k] else 1
                        return block_of(pack[2 + axis, ks.index(k)], half)

                    place(5 + axis, i, k, row_on, own_lanes, block)
                received = pack[2 + axis, ks.index(BACK[i])]
                as_rows = own_rows if axis == 0 else z_rows
                weigh(5 + axis, as_rows, block_of(received, 1), own_cols)

    chunk = n_ao // PARTS
    high = chunk * slab

    def t_copy(to, p, lanes):
        source, target = 0, 1 + to
        if to < 2:
            gk, ak = shifted(1 - 2 * to, 0, 0)
        elif to == 3 and p < PARTS // 2:
            gk, ak = along(1, -1)
            source, target = target, source
        else:
            gk, ak = along(to - 2, 1)
        if lanes:
            here = tn.at[source, pl.ds(p * high, high), pl.ds(0, main)]
            there = tn.at[target, pl.ds(p * high, high), pl.ds(0, main)]
        else:
            here = tt.at[source, pl.ds(p * high // 2, high // 2)]
            there = tt.at[target, pl.ds(p * high // 2, high // 2)]
        return pltpu.make_async_remote_copy(
            src_ref=here,
            dst_ref=there,
            send_sem=ex_send.at[to, p, lanes],
            recv_sem=ex_recv.at[to, p, lanes],
            device_id={"ao": ak, "grp": gk},
            device_id_type=MESH,
        )

    t_copies = [[[t_copy(to, p, lanes) for lanes in range(2)] for p in range(PARTS)] for to in range(4)]

    def unpack_tail(at, p):
        last = tt[at, p * high // 2 : (p + 1) * high // 2, :].astype(F32)
        last = last.reshape(line // PARTS, deep, 2 * bs)
        both = jnp.concatenate([last[:, :, :bs], last[:, :, bs:]], axis=1)
        tn[at, p * high : (p + 1) * high, main:] = both.reshape(high, bs).astype(BF16)

    def take_part(p, slot, on_to):
        lacks = p % 2
        arrived = arr.at[pl.ds(p * chunk, chunk - lacks)]
        pltpu.make_async_copy(arrived, arrived, a2a_recv.at[p]).wait()
        tn[slot, p * high : (p + 1) * high, :main] = (
            arr[p * chunk : (p + 1) * chunk].astype(F32).reshape(high, main).astype(BF16)
        )
        for to in on_to:
            t_copies[to][p][1].start()
        arrived = tt.at[slot, pl.ds(p * high // 2, (line // PARTS - lacks) * deep)]
        pltpu.make_async_copy(arrived, arrived, z_recv.at[p]).wait()
        for to in on_to:
            t_copies[to][p][0].start()
        unpack_tail(slot, p)

    for p in range(PARTS // 2):
        take_part(p, 4, (3,))
    for p in range(PARTS // 2):
        for lanes in (1, 0):
            t_copies[3][p][lanes].wait_recv()
            for to in (2, 1, 0):
                t_copies[to][p][lanes].start()
        unpack_tail(0, p)
    for p in range(PARTS // 2, PARTS):
        take_part(p, 0, (3, 2, 1, 0))

    for s in range(5):
        xs[s] = jnp.dot(tn[0], vs[s], preferred_element_type=F32).astype(BF16)

    def pair_sum(slot, left, right, r0, r1_, c0, c1):
        pairs = lax.dot_general(left, right, (((1,), (1,)), ((), ())), preferred_element_type=F32)
        weighted = pairs * oexp[slot, r0:r1_, c0:c1]
        summed = jnp.sum(weighted.reshape((r1_ - r0) // slab, slab, c1 - c0), axis=0)
        folded = summed[:, 0:128]
        for at in range(1, (c1 - c0) // 128):
            folded = folded + summed[:, at * 128 : (at + 1) * 128]
        return folded

    part_sum = pair_sum(0, xs[0], tn[0], 0, tall, 0, tall)
    early = (PARTS - 1) * high
    for lo, hi, parts in ((0, early, range(PARTS - 1)), (early, tall, (PARTS - 1,))):
        for to in (0, 1, 2, 3):
            for p in parts:
                if to < 3 or p >= PARTS // 2:
                    for copy in t_copies[to][p]:
                        copy.wait_recv()
        for to in (0, 1, 2, 3):
            for p in parts:
                if to < 3 or p >= PARTS // 2:
                    unpack_tail(1 + to, p)
        both = {}
        for to in (2, 3):
            both[to] = jnp.dot(
                tn[1 + to, lo:hi, :], vs[3 + to], preferred_element_type=F32
            ).astype(BF16)
        for to in (0, 1, 2, 3):
            part_sum = part_sum + pair_sum(
                1 + to, xs[1 + to], tn[1 + to, lo:hi, :], 0, tall, lo, hi
            )
        for to in (2, 3):
            part_sum = part_sum + pair_sum(3 + to, both[to], tn[0], lo, hi, 0, tall)

    shift = 64
    while shift >= slab:
        part_sum = part_sum + pltpu.roll(part_sum, shift, 1)
        shift //= 2

    def left_all():
        for copy in v_copies + p_copies + [c for per in t_copies for two in per for c in two]:
            copy.wait_send()
        wait_bytes(snd, n_ao - 1, a2a_send)
        wait_bytes(y_out, rows, y_send)
        wait_bytes(z_out, line - 1, z_send)

    for p in range(slab):
        psend[p] = part_sum[p : p + 1, :]

    def all_slots(buf, count):
        acc = buf[0]
        for at in range(1, count):
            acc = acc + buf[at]
        return acc

    for dg in (4, 3, 5, 2, 6, 1, 7, 0):
        gg = lax.rem(g + dg, groups)
        for q in (1, 0, 2, 3):
            if dg or q < rows - 1:
                pltpu.make_async_remote_copy(
                    src_ref=psend.at[gg],
                    dst_ref=r1.at[g * rows + y],
                    send_sem=r_send.at[0],
                    recv_sem=r_recv.at[0],
                    device_id={"ao": y_at[q] * line + z, "grp": gg},
                    device_id_type=MESH,
                ).start()
    r1[g * rows + y] = psend[g]
    wait_bytes(r1, groups * rows, r_recv.at[0])
    r3[z] = all_slots(r1, groups * rows)

    def to_line(z_to):
        pltpu.make_async_remote_copy(
            src_ref=r3.at[z],
            dst_ref=r3.at[z],
            send_sem=r_send.at[1],
            recv_sem=r_recv.at[1],
            device_id={"ao": y * line + z_to, "grp": g},
            device_id_type=MESH,
        ).start()

    def to_both_ways(i, carry):
        for z_to, _ in both_ways(i):
            to_line(z_to)
        return carry

    to_line(across_line)
    lax.fori_loop(1, half_line, to_both_ways, 0)
    left_all()
    wait_bytes(r1, groups * rows, r_send.at[0])
    wait_bytes(r3, line, r_recv.at[1])
    scale = 1.0 / (bs * math.sqrt(groups * n_ao))
    out_ref[...] = (all_slots(r3, line) * scale)[:, :slab]
    wait_bytes(r3, line, r_send.at[1])


def body(three_center, occ_density, virt_density, tensor_mask, occ_mask, virt_mask, block_sizes):
    groups = lax.axis_size("grp")
    n_ao = lax.axis_size("ao")
    rows = 4
    line = n_ao // rows
    slab = three_center.shape[0]
    bs = occ_density.shape[2]
    width = 7 * bs
    tall = bs * slab
    dims = (groups, rows, line, slab, bs)
    dma = pltpu.SemaphoreType.DMA
    result = pl.pallas_call(
        functools.partial(kernel, dims),
        out_shape=jax.ShapeDtypeStruct((1, slab), F32),
        in_specs=[pl.BlockSpec(memory_space=pltpu.HBM)] * 7,
        out_specs=pl.BlockSpec(memory_space=pltpu.VMEM),
        scratch_shapes=[
            pltpu.VMEM((slab, n_ao, width), BF16),
            pltpu.VMEM((bs, width), BF16),
            pltpu.VMEM((bs, width), BF16),
            pltpu.SMEM((7, groups, n_ao), jnp.int32),
            pltpu.SMEM((7, groups, n_ao), jnp.int32),
            pltpu.SMEM((7, groups, n_ao), jnp.int32),
            pltpu.SMEM((groups, n_ao), jnp.int32),
            dma((7,)),
            pltpu.VMEM((n_ao, slab, width // 128 * 128), BF16),
            pltpu.VMEM((n_ao, slab, width // 128 * 128), BF16),
            pltpu.VMEM((5, tall, width), BF16),
            pltpu.VMEM((7, bs, width), BF16),
            pltpu.VMEM((4, 5, bs, 2 * bs), BF16),
            pltpu.VMEM((7, width, width), BF16),
            pltpu.VMEM((5, tall, width), BF16),
            pltpu.VMEM((7, tall, tall), F32),
            pltpu.VMEM((slab, 1, 128), F32),
            pltpu.VMEM((groups * rows, 1, 128), F32),
            pltpu.VMEM((line, 1, 128), F32),
            pltpu.VMEM((rows, bs, 2 * bs), BF16),
            pltpu.VMEM((rows, bs, 2 * bs), BF16),
            pltpu.VMEM((line, 2 * slab, 2 * bs), BF16),
            pltpu.VMEM((5, line * 2 * slab, 2 * bs), BF16),
            dma,
            dma((PARTS,)),
            dma,
            dma,
            dma,
            dma((PARTS,)),
            dma((4, PARTS, 2)),
            dma((4, PARTS, 2)),
            dma((6,)),
            dma((6,)),
            dma((2,)),
            dma((2,)),
            dma((2,)),
            dma((2,)),
        ],
        compiler_params=pltpu.CompilerParams(
            collective_id=0, has_side_effects=True, vmem_limit_bytes=60 * 1024 * 1024
        ),
    )(
        three_center,
        occ_density.reshape(bs, width),
        virt_density.reshape(bs, width),
        jnp.transpose(tensor_mask, (2, 0, 1)),
        jnp.transpose(occ_mask, (2, 0, 1)),
        jnp.transpose(virt_mask, (2, 0, 1)),
        block_sizes,
    )
    return result


def solution(mesh):
    in_specs = (
        P(None, "grp", "ao"),
        P("grp", "ao", None, None),
        P("grp", "ao", None, None),
        P(),
        P(),
        P(),
        P(),
    )
    return jax.shard_map(
        body, mesh=mesh, in_specs=in_specs, out_specs=P("grp", None), check_vma=False
    )
```

```python
import functools
import math

import jax
import jax.numpy as jnp
from jax import lax
from jax.experimental import pallas as pl
from jax.experimental.pallas import tpu as pltpu
from jax.sharding import PartitionSpec as P

MESH = pl.DeviceIdType.MESH
BF16 = jnp.bfloat16
F32 = jnp.float32
STEPS = ((0, 0, 0), (-1, 0, 0), (1, 0, 0), (0, -1, 0), (0, 1, 0), (0, 0, -1), (0, 0, 1))
BACK = (0, 2, 1, 4, 3, 6, 5)
PARTS = 4


def second_step(i, j, k):
    want = tuple(STEPS[i][x] + STEPS[j][x] - STEPS[k][x] for x in range(3))
    return STEPS.index(want) if want in STEPS else None


def kernel(
    dims,
    t_hbm,
    occ_hbm,
    virt_hbm,
    tm_hbm,
    om_hbm,
    vm_hbm,
    sz_hbm,
    out_ref,
    t_ref,
    occ_ref,
    virt_ref,
    tm_ref,
    om_ref,
    vm_ref,
    sz_ref,
    load_sem,
    snd,
    arr,
    tn,
    vn,
    pack,
    vs,
    xs,
    oexp,
    psend,
    r1,
    r3,
    y_out,
    y_in,
    z_out,
    tt,
    a2a_send,
    a2a_recv,
    y_send,
    y_recv,
    z_send,
    z_recv,
    ex_send,
    ex_recv,
    v_send,
    v_recv,
    p_send,
    p_recv,
    r_send,
    r_recv,
):
    groups, rows, line, slab, bs = dims
    n_ao = rows * line
    width = 7 * bs
    tall = bs * slab
    main = width // 128 * 128
    g = lax.axis_index("grp")
    a = lax.axis_index("ao")
    y = a // line
    z = a % line
    odd = g % 2
    way = 1 - 2 * odd

    def shifted(dg, dy, dz):
        gg = (g + dg + groups) % groups
        yy = (y + dy + rows) % rows
        zz = (z + dz + line) % line
        return gg, yy * line + zz

    def exists(first, second=(0, 0, 0)):
        gg = g + first[0] + second[0]
        yy = y + first[1] + second[1]
        zz = z + first[2] + second[2]
        inside = (gg >= 0) & (gg < groups) & (yy >= 0) & (yy < rows) & (zz >= 0) & (zz < line)
        return inside.astype(jnp.int32)

    loads = []
    for at, (source, target) in enumerate(
        (
            (t_hbm, t_ref),
            (virt_hbm, virt_ref),
            (vm_hbm, vm_ref),
            (sz_hbm, sz_ref),
            (occ_hbm, occ_ref),
            (om_hbm, om_ref),
            (tm_hbm, tm_ref),
        )
    ):
        loads.append(pltpu.make_async_copy(source, target, load_sem.at[at]))
        loads[-1].start()

    barrier = pltpu.get_barrier_semaphore()
    half_line = line // 2
    y_at = [lax.rem(y + rows - 1 - q, rows) for q in range(rows)]
    across_line = lax.rem(z + half_line, line)

    def both_ways(i):
        far = half_line - i
        return (
            (lax.rem(z + far, line), 2 * i - 1),
            (lax.rem(z - far + line, line), 2 * i),
        )

    def greet(aa, gg):
        pl.semaphore_signal(barrier, inc=1, device_id={"ao": aa, "grp": gg}, device_id_type=MESH)

    for q in range(rows):
        greet(y_at[q] * line + across_line, g)

    def greet_ao(i, carry):
        for z_to, _ in both_ways(i):
            for q in range(rows):
                greet(y_at[q] * line + z_to, g)
        return carry

    lax.fori_loop(1, half_line, greet_ao, 0)
    for q in range(rows - 1):
        greet(y_at[q] * line + z, g)

    def greet_sheet(d, carry):
        gg = lax.rem(g + d, groups)
        for q in range(rows):
            greet(y_at[q] * line + z, gg)
        return carry

    lax.fori_loop(1, groups, greet_sheet, 0)

    lane = lax.broadcasted_iota(jnp.int32, (1, width), 1)
    lane_block = lane // bs
    lane_in = lane % bs
    row_at = lax.broadcasted_iota(jnp.int32, (bs, 1), 0)

    def masked(density, mask_ref):
        bound = jnp.zeros((1, width), jnp.int32)
        for k in range(7):
            gk, ak = shifted(*STEPS[k])
            value = sz_ref[gk, ak] * mask_ref[k, g, a] * exists(STEPS[k])
            bound = bound + jnp.where(lane_block == k, value, 0)
        keep_col = jnp.where(lane_in < bound, 1.0, 0.0)
        keep_row = jnp.where(row_at < sz_ref[g, a], 1.0, 0.0)
        return (density.astype(F32) * (keep_row * keep_col)).astype(BF16)

    for at in (1, 2, 3):
        loads[at].wait()
    vn[0] = masked(virt_ref[...], vm_ref)

    loads[0].wait()
    part = n_ao // 2
    n_rows = part * slab
    to = lax.broadcasted_iota(jnp.int32, (n_rows, n_rows), 0)
    frm = lax.broadcasted_iota(jnp.int32, (n_rows, n_rows), 1)
    perm = jnp.where(frm == (to % slab) * part + to // slab, 1.0, 0.0).astype(BF16)
    for half in range(2):
        rows_in = t_ref[:, half * part : (half + 1) * part, :].reshape(n_rows, width)
        moved_rows = jnp.dot(perm, rows_in, preferred_element_type=F32)
        snd[half * part : (half + 1) * part] = (
            moved_rows[:, :main].reshape(part, slab, main).astype(BF16)
        )
        for at in range(rows // 2):
            first = moved_rows[at * 2 * bs : at * 2 * bs + bs, main:]
            second = moved_rows[at * 2 * bs + bs : at * 2 * bs + 2 * bs, main:]
            y_out[half * (rows // 2) + at] = jnp.concatenate([first, second], axis=1).astype(BF16)

    pl.semaphore_wait(barrier, n_ao - 1 + (groups - 1) * rows)

    def v_copy(k):
        gk, ak = shifted(*(-x for x in STEPS[k]))
        return pltpu.make_async_remote_copy(
            src_ref=vn.at[0],
            dst_ref=vn.at[k],
            send_sem=v_send.at[k - 1],
            recv_sem=v_recv.at[k - 1],
            device_id={"ao": ak, "grp": gk},
            device_id_type=MESH,
        )

    def give_y(q):
        return pltpu.make_async_remote_copy(
            src_ref=y_out.at[y_at[q]],
            dst_ref=y_in.at[y],
            send_sem=y_send,
            recv_sem=y_recv,
            device_id={"ao": y_at[q] * line + z, "grp": g},
            device_id_type=MESH,
        )

    for q in range(rows - 1):
        give_y(q).start()

    def place_at(steps):
        return lax.rem(z + way * steps + line, line)

    def give(turn, z_to, z_block, count=rows):
        for q in range(count):
            pltpu.make_async_remote_copy(
                src_ref=snd.at[y_at[q] * line + z_block],
                dst_ref=arr.at[turn * rows + y],
                send_sem=a2a_send,
                recv_sem=a2a_recv.at[turn // (line // PARTS)],
                device_id={"ao": y_at[q] * line + z_to, "grp": g},
                device_id_type=MESH,
            ).start()

    def give_ahead(turn, carry):
        far = half_line - 1 - turn
        give(turn, place_at(-far), place_at(-far - 1))
        return carry

    def give_own(turn, carry):
        z_to = place_at(line - 1 - turn)
        give(turn, z_to, z_to)
        return carry

    v_copies = [v_copy(k) for k in range(1, 7)]
    for copy in v_copies:
        copy.start()
    lax.fori_loop(0, 4, give_ahead, 0)
    arr[(half_line - 1) * rows + y] = snd[y * line + place_at(-1)]
    arr[n_ao - rows + y] = snd[a]
    y_in[y] = y_out[y]

    for at in (4, 5, 6):
        loads[at].wait()
    occ = masked(occ_ref[...], om_ref)

    def wait_bytes(buf, count, sem):
        ref = buf.at[pl.ds(0, count - 1)]
        pltpu.make_async_copy(ref, ref, sem).wait()

    wait_bytes(y_in, rows, y_recv)
    for half in range(2):
        pieces = [y_in[at][:, half * bs : (half + 1) * bs].astype(F32) for at in range(rows)]
        upper = jnp.concatenate([pieces[0], pieces[2]], axis=1).reshape(line // 2, slab, 2 * bs)
        lower = jnp.concatenate([pieces[1], pieces[3]], axis=1).reshape(line // 2, slab, 2 * bs)
        z_out[half * (line // 2) : (half + 1) * (line // 2)] = jnp.concatenate(
            [upper, lower], axis=1
        ).astype(BF16)
    deep = 2 * slab

    def give_z(slot, turn, z_to, z_block):
        pltpu.make_async_remote_copy(
            src_ref=z_out.at[z_block],
            dst_ref=tt.at[slot, pl.ds(pl.multiple_of(turn * deep, deep), deep)],
            send_sem=z_send,
            recv_sem=z_recv.at[turn // (line // PARTS)],
            device_id={"ao": y * line + z_to, "grp": g},
            device_id_type=MESH,
        ).start()

    def give_z_ahead(turn, carry):
        far = half_line - 1 - turn
        give_z(4, turn, place_at(-far), place_at(-far - 1))
        return carry

    def give_z_own(turn, carry):
        z_to = place_at(line - 1 - turn)
        give_z(0, turn, z_to, z_to)
        return carry

    lax.fori_loop(0, half_line - 1, give_z_ahead, 0)
    lax.fori_loop(half_line, line - 1, give_z_own, 0)
    tt[4, (half_line - 1) * deep : half_line * deep] = z_out[place_at(-1)]
    tt[0, (line - 1) * deep : line * deep] = z_out[z]

    for copy in v_copies:
        copy.wait_recv()

    def towards(parity, axis):
        return (4 if parity == 0 else 3) if axis == 0 else (6 if parity == 0 else 5)

    def others(step):
        return [k for k in range(1, 7) if k != step]

    def block_of(value, k):
        return value[:, k * bs : (k + 1) * bs]

    for parity in range(2):

        @pl.when(odd == parity)
        def _(parity=parity):
            for axis in range(2):
                step = towards(parity, axis)
                for at, k in enumerate(others(step)):
                    here = block_of(vn[k], BACK[k])
                    there = block_of(occ if k == BACK[step] else vn[k], step)
                    pack[axis, at] = jnp.concatenate([here, there], axis=1)

    def along(axis, sign):
        return shifted(0, sign * way, 0) if axis == 0 else shifted(0, 0, sign * way)

    def p_copy(axis):
        gk, ak = along(axis, 1)
        return pltpu.make_async_remote_copy(
            src_ref=pack.at[axis],
            dst_ref=pack.at[2 + axis],
            send_sem=p_send.at[axis],
            recv_sem=p_recv.at[axis],
            device_id={"ao": ak, "grp": gk},
            device_id_type=MESH,
        )

    p_copies = [p_copy(axis) for axis in range(2)]
    for copy in p_copies:
        copy.start()
    lax.fori_loop(4, half_line - 1, give_ahead, 0)
    give(half_line - 1, z, place_at(-1), rows - 1)

    chunk = n_ao // PARTS
    high = chunk * slab

    def t_copy(to, p, lanes):
        source, target = 0, 1 + to
        if to < 2:
            gk, ak = shifted(1 - 2 * to, 0, 0)
        elif to == 3 and p < PARTS // 2:
            gk, ak = along(1, -1)
            source, target = target, source
        else:
            gk, ak = along(to - 2, 1)
        if lanes:
            here = tn.at[source, pl.ds(p * high, high), pl.ds(0, main)]
            there = tn.at[target, pl.ds(p * high, high), pl.ds(0, main)]
        else:
            here = tt.at[source, pl.ds(p * high // 2, high // 2)]
            there = tt.at[target, pl.ds(p * high // 2, high // 2)]
        return pltpu.make_async_remote_copy(
            src_ref=here,
            dst_ref=there,
            send_sem=ex_send.at[to, p, lanes],
            recv_sem=ex_recv.at[to, p, lanes],
            device_id={"ao": ak, "grp": gk},
            device_id_type=MESH,
        )

    t_copies = [[[t_copy(to, p, lanes) for lanes in range(2)] for p in range(PARTS)] for to in range(4)]

    def unpack_tail(at, p):
        last = tt[at, p * high // 2 : (p + 1) * high // 2, :].astype(F32)
        last = last.reshape(line // PARTS, deep, 2 * bs)
        both = jnp.concatenate([last[:, :, :bs], last[:, :, bs:]], axis=1)
        tn[at, p * high : (p + 1) * high, main:] = both.reshape(high, bs).astype(BF16)

    def take_part(p, slot, on_to):
        lacks = p % 2
        arrived = arr.at[pl.ds(p * chunk, chunk - lacks)]
        pltpu.make_async_copy(arrived, arrived, a2a_recv.at[p]).wait()
        tn[slot, p * high : (p + 1) * high, :main] = (
            arr[p * chunk : (p + 1) * chunk].astype(F32).reshape(high, main).astype(BF16)
        )
        for to in on_to:
            t_copies[to][p][1].start()
        arrived = tt.at[slot, pl.ds(p * high // 2, (line // PARTS - lacks) * deep)]
        pltpu.make_async_copy(arrived, arrived, z_recv.at[p]).wait()
        for to in on_to:
            t_copies[to][p][0].start()
        unpack_tail(slot, p)

    def pass_ahead_part(p):
        for lanes in (1, 0):
            t_copies[3][p][lanes].wait_recv()
            for to in (2, 1, 0):
                t_copies[to][p][lanes].start()
        unpack_tail(0, p)

    def mask_lanes(block_step):
        gi, ai = shifted(*block_step)
        on = jnp.zeros((1, width), jnp.int32)
        for j in range(7):
            value = tm_ref[j, gi, ai] * exists(block_step, STEPS[j])
            on = on + jnp.where(lane_block == j, value, 0)
        return on.astype(F32)

    own_lanes = mask_lanes(STEPS[0])
    nothing = jnp.zeros((bs, bs), F32)

    def place(slot, i, k, row_on, lanes_on, block):
        pieces = []
        for j in range(7):
            k2 = second_step(i, j, k)
            pieces.append(nothing if k2 is None else block(k2).astype(F32))
        placed = jnp.concatenate(pieces, axis=1) * lanes_on * row_on
        vs[slot, k * bs : (k + 1) * bs, :] = placed.astype(BF16)

    def place_all(slot_steps):
        lanes = [mask_lanes(STEPS[i]) for _, i in slot_steps]
        for k in range(7):
            row_on = (tm_ref[k, g, a] * exists(STEPS[k])).astype(F32)
            for (slot, i), lanes_on in zip(slot_steps, lanes):
                place(slot, i, k, row_on, lanes_on, lambda k2: block_of(vn[k], k2))

    lax.fori_loop(8, 10, give_own, 0)
    place_all([(0, 0), (1, 1), (2, 2)])
    for parity in range(2):

        @pl.when(odd == parity)
        def _(parity=parity):
            place_all([(3, BACK[towards(parity, 0)]), (4, BACK[towards(parity, 1)])])

    take_part(0, 4, (3,))
    lax.fori_loop(10, 12, give_own, 0)
    def source_of(slot, zz, ww):
        turn = slot >> 2
        ahead = jnp.where(turn < half_line, half_line - turn, turn - (line - 1))
        return (slot & (rows - 1)) * line + ((zz + ww * ahead + line) & (line - 1))

    def spread(zz, ww):
        down = lax.broadcasted_iota(jnp.int32, (tall, bs), 0) // slab
        across = lax.broadcasted_iota(jnp.int32, (bs, tall), 1) // slab
        tall_at = lax.broadcasted_iota(jnp.int32, (tall, bs), 1)
        wide_at = lax.broadcasted_iota(jnp.int32, (bs, tall), 0)
        as_rows = jnp.where(source_of(down, zz, ww) == tall_at, 1.0, 0.0).astype(BF16)
        as_cols = jnp.where(source_of(across, zz, ww) == wide_at, 1.0, 0.0).astype(BF16)
        return as_rows, as_cols

    own_rows, own_cols = spread(z, way)
    x_cols = spread(z, -way)[1]
    z_rows, z_cols = spread(place_at(-1), way)

    def weigh(slot, as_rows, block, as_cols):
        stretched = jnp.dot(as_rows, block, preferred_element_type=F32).astype(BF16)
        oexp[slot] = jnp.dot(stretched, as_cols, preferred_element_type=F32)

    def by_way(up, down):
        keep = odd.astype(F32)
        both = block_of(occ, up).astype(F32) * (1.0 - keep) + block_of(occ, down).astype(F32) * keep
        return both.astype(BF16)

    weigh(0, own_rows, block_of(occ, 0), own_cols)
    weigh(1, own_rows, block_of(occ, 1), x_cols)
    weigh(2, own_rows, block_of(occ, 2), x_cols)
    weigh(3, own_rows, by_way(3, 4), own_cols)
    weigh(4, own_rows, by_way(5, 6), z_cols)

    take_part(1, 4, (3,))
    lax.fori_loop(12, 15, give_own, 0)
    give(line - 1, z, z, rows - 1)
    for axis in range(2):
        p_copies[axis].wait_recv()
    for parity in range(2):

        @pl.when(odd == parity)
        def _(parity=parity):
            for axis in range(2):
                i = towards(parity, axis)
                ks = others(i)
                source = STEPS[BACK[i]]
                gs, a_s = shifted(*source)
                for k in range(7):
                    row_on = (tm_ref[k, gs, a_s] * exists(source, STEPS[k])).astype(F32)

                    def block(k2, k=k):
                        if k == 0:
                            return block_of(vn[BACK[i]], k2)
                        if k == i:
                            return block_of(vn[0], k2)
                        half = 0 if k2 == BACK[k] else 1
                        return block_of(pack[2 + axis, ks.index(k)], half)

                    place(5 + axis, i, k, row_on, own_lanes, block)
                received = pack[2 + axis, ks.index(BACK[i])]
                as_rows = own_rows if axis == 0 else z_rows
                weigh(5 + axis, as_rows, block_of(received, 1), own_cols)

    pass_ahead_part(0)
    pass_ahead_part(1)
    for p in range(PARTS // 2, PARTS):
        take_part(p, 0, (3, 2, 1, 0))

    for s in range(5):
        xs[s] = jnp.dot(tn[0], vs[s], preferred_element_type=F32).astype(BF16)

    def pair_sum(slot, left, right, r0, r1_, c0, c1):
        pairs = lax.dot_general(left, right, (((1,), (1,)), ((), ())), preferred_element_type=F32)
        weighted = pairs * oexp[slot, r0:r1_, c0:c1]
        summed = jnp.sum(weighted.reshape((r1_ - r0) // slab, slab, c1 - c0), axis=0)
        folded = summed[:, 0:128]
        for at in range(1, (c1 - c0) // 128):
            folded = folded + summed[:, at * 128 : (at + 1) * 128]
        return folded

    part_sum = pair_sum(0, xs[0], tn[0], 0, tall, 0, tall)
    early = (PARTS - 1) * high
    for lo, hi, parts in ((0, early, range(PARTS - 1)), (early, tall, (PARTS - 1,))):
        for to in (0, 1, 2, 3):
            for p in parts:
                if to < 3 or p >= PARTS // 2:
                    for copy in t_copies[to][p]:
                        copy.wait_recv()
        for to in (0, 1, 2, 3):
            for p in parts:
                if to < 3 or p >= PARTS // 2:
                    unpack_tail(1 + to, p)
        both = {}
        for to in (2, 3):
            both[to] = jnp.dot(
                tn[1 + to, lo:hi, :], vs[3 + to], preferred_element_type=F32
            ).astype(BF16)
        for to in (0, 1, 2, 3):
            part_sum = part_sum + pair_sum(
                1 + to, xs[1 + to], tn[1 + to, lo:hi, :], 0, tall, lo, hi
            )
        for to in (2, 3):
            part_sum = part_sum + pair_sum(3 + to, both[to], tn[0], lo, hi, 0, tall)

    shift = 64
    while shift >= slab:
        part_sum = part_sum + pltpu.roll(part_sum, shift, 1)
        shift //= 2

    def left_all():
        for copy in v_copies + p_copies + [c for per in t_copies for two in per for c in two]:
            copy.wait_send()
        wait_bytes(snd, n_ao - 1, a2a_send)
        wait_bytes(y_out, rows, y_send)
        wait_bytes(z_out, line - 1, z_send)

    for p in range(slab):
        psend[p] = part_sum[p : p + 1, :]

    def all_slots(buf, count):
        acc = buf[0]
        for at in range(1, count):
            acc = acc + buf[at]
        return acc

    for dg in (4, 3, 5, 2, 6, 1, 7, 0):
        gg = lax.rem(g + dg, groups)
        for q in (1, 0, 2, 3):
            if dg or q < rows - 1:
                pltpu.make_async_remote_copy(
                    src_ref=psend.at[gg],
                    dst_ref=r1.at[g * rows + y],
                    send_sem=r_send.at[0],
                    recv_sem=r_recv.at[0],
                    device_id={"ao": y_at[q] * line + z, "grp": gg},
                    device_id_type=MESH,
                ).start()
    r1[g * rows + y] = psend[g]
    wait_bytes(r1, groups * rows, r_recv.at[0])
    r3[z] = all_slots(r1, groups * rows)

    def to_line(z_to):
        pltpu.make_async_remote_copy(
            src_ref=r3.at[z],
            dst_ref=r3.at[z],
            send_sem=r_send.at[1],
            recv_sem=r_recv.at[1],
            device_id={"ao": y * line + z_to, "grp": g},
            device_id_type=MESH,
        ).start()

    def to_both_ways(i, carry):
        for z_to, _ in both_ways(i):
            to_line(z_to)
        return carry

    to_line(across_line)
    lax.fori_loop(1, half_line, to_both_ways, 0)
    left_all()
    wait_bytes(r1, groups * rows, r_send.at[0])
    wait_bytes(r3, line, r_recv.at[1])
    scale = 1.0 / (bs * math.sqrt(groups * n_ao))
    out_ref[...] = (all_slots(r3, line) * scale)[:, :slab]
    wait_bytes(r3, line, r_send.at[1])


def body(three_center, occ_density, virt_density, tensor_mask, occ_mask, virt_mask, block_sizes):
    groups = lax.axis_size("grp")
    n_ao = lax.axis_size("ao")
    rows = 4
    line = n_ao // rows
    slab = three_center.shape[0]
    bs = occ_density.shape[2]
    width = 7 * bs
    tall = bs * slab
    dims = (groups, rows, line, slab, bs)
    dma = pltpu.SemaphoreType.DMA
    result = pl.pallas_call(
        functools.partial(kernel, dims),
        out_shape=jax.ShapeDtypeStruct((1, slab), F32),
        in_specs=[pl.BlockSpec(memory_space=pltpu.HBM)] * 7,
        out_specs=pl.BlockSpec(memory_space=pltpu.VMEM),
        scratch_shapes=[
            pltpu.VMEM((slab, n_ao, width), BF16),
            pltpu.VMEM((bs, width), BF16),
            pltpu.VMEM((bs, width), BF16),
            pltpu.SMEM((7, groups, n_ao), jnp.int32),
            pltpu.SMEM((7, groups, n_ao), jnp.int32),
            pltpu.SMEM((7, groups, n_ao), jnp.int32),
            pltpu.SMEM((groups, n_ao), jnp.int32),
            dma((7,)),
            pltpu.VMEM((n_ao, slab, width // 128 * 128), BF16),
            pltpu.VMEM((n_ao, slab, width // 128 * 128), BF16),
            pltpu.VMEM((5, tall, width), BF16),
            pltpu.VMEM((7, bs, width), BF16),
            pltpu.VMEM((4, 5, bs, 2 * bs), BF16),
            pltpu.VMEM((7, width, width), BF16),
            pltpu.VMEM((5, tall, width), BF16),
            pltpu.VMEM((7, tall, tall), F32),
            pltpu.VMEM((slab, 1, 128), F32),
            pltpu.VMEM((groups * rows, 1, 128), F32),
            pltpu.VMEM((line, 1, 128), F32),
            pltpu.VMEM((rows, bs, 2 * bs), BF16),
            pltpu.VMEM((rows, bs, 2 * bs), BF16),
            pltpu.VMEM((line, 2 * slab, 2 * bs), BF16),
            pltpu.VMEM((5, line * 2 * slab, 2 * bs), BF16),
            dma,
            dma((PARTS,)),
            dma,
            dma,
            dma,
            dma((PARTS,)),
            dma((4, PARTS, 2)),
            dma((4, PARTS, 2)),
            dma((6,)),
            dma((6,)),
            dma((2,)),
            dma((2,)),
            dma((2,)),
            dma((2,)),
        ],
        compiler_params=pltpu.CompilerParams(
            collective_id=0, has_side_effects=True, vmem_limit_bytes=60 * 1024 * 1024
        ),
    )(
        three_center,
        occ_density.reshape(bs, width),
        virt_density.reshape(bs, width),
        jnp.transpose(tensor_mask, (2, 0, 1)),
        jnp.transpose(occ_mask, (2, 0, 1)),
        jnp.transpose(virt_mask, (2, 0, 1)),
        block_sizes,
    )
    return result


def solution(mesh):
    in_specs = (
        P(None, "grp", "ao"),
        P("grp", "ao", None, None),
        P("grp", "ao", None, None),
        P(),
        P(),
        P(),
        P(),
    )
    return jax.shard_map(
        body, mesh=mesh, in_specs=in_specs, out_specs=P("grp", None), check_vma=False
    )
```

```python
import functools
import math

import jax
import jax.numpy as jnp
from jax import lax
from jax.experimental import pallas as pl
from jax.experimental.pallas import tpu as pltpu
from jax.sharding import PartitionSpec as P

MESH = pl.DeviceIdType.MESH
BF16 = jnp.bfloat16
F32 = jnp.float32
STEPS = ((0, 0, 0), (-1, 0, 0), (1, 0, 0), (0, -1, 0), (0, 1, 0), (0, 0, -1), (0, 0, 1))
BACK = (0, 2, 1, 4, 3, 6, 5)
PARTS = 4


def second_step(i, j, k):
    want = tuple(STEPS[i][x] + STEPS[j][x] - STEPS[k][x] for x in range(3))
    return STEPS.index(want) if want in STEPS else None


def kernel(
    dims,
    t_hbm,
    occ_hbm,
    virt_hbm,
    tm_hbm,
    om_hbm,
    vm_hbm,
    sz_hbm,
    out_ref,
    t_ref,
    occ_ref,
    virt_ref,
    tm_ref,
    om_ref,
    vm_ref,
    sz_ref,
    load_sem,
    snd,
    arr,
    tn,
    vn,
    pack,
    vs,
    xs,
    oexp,
    psend,
    r1,
    r3,
    y_out,
    y_in,
    z_out,
    tt,
    a2a_send,
    a2a_recv,
    y_send,
    y_recv,
    z_send,
    z_recv,
    ex_send,
    ex_recv,
    v_send,
    v_recv,
    p_send,
    p_recv,
    r_send,
    r_recv,
):
    groups, rows, line, slab, bs = dims
    n_ao = rows * line
    width = 7 * bs
    tall = bs * slab
    main = width // 128 * 128
    g = lax.axis_index("grp")
    a = lax.axis_index("ao")
    y = a // line
    z = a % line
    odd = g % 2
    way = 1 - 2 * odd

    def shifted(dg, dy, dz):
        gg = (g + dg + groups) % groups
        yy = (y + dy + rows) % rows
        zz = (z + dz + line) % line
        return gg, yy * line + zz

    def exists(first, second=(0, 0, 0)):
        gg = g + first[0] + second[0]
        yy = y + first[1] + second[1]
        zz = z + first[2] + second[2]
        inside = (gg >= 0) & (gg < groups) & (yy >= 0) & (yy < rows) & (zz >= 0) & (zz < line)
        return inside.astype(jnp.int32)

    loads = []
    for at, (source, target) in enumerate(
        (
            (t_hbm, t_ref),
            (virt_hbm, virt_ref),
            (vm_hbm, vm_ref),
            (sz_hbm, sz_ref),
            (occ_hbm, occ_ref),
            (om_hbm, om_ref),
            (tm_hbm, tm_ref),
        )
    ):
        loads.append(pltpu.make_async_copy(source, target, load_sem.at[at]))
        loads[-1].start()

    barrier = pltpu.get_barrier_semaphore()
    half_line = line // 2
    y_at = [lax.rem(y + rows - 1 - q, rows) for q in range(rows)]
    across_line = lax.rem(z + half_line, line)

    def both_ways(i):
        far = half_line - i
        return (
            (lax.rem(z + far, line), 2 * i - 1),
            (lax.rem(z - far + line, line), 2 * i),
        )

    def greet(aa, gg):
        pl.semaphore_signal(barrier, inc=1, device_id={"ao": aa, "grp": gg}, device_id_type=MESH)

    for q in range(rows):
        greet(y_at[q] * line + across_line, g)

    def greet_ao(i, carry):
        for z_to, _ in both_ways(i):
            for q in range(rows):
                greet(y_at[q] * line + z_to, g)
        return carry

    lax.fori_loop(1, half_line, greet_ao, 0)
    for q in range(rows - 1):
        greet(y_at[q] * line + z, g)

    def greet_sheet(d, carry):
        gg = lax.rem(g + d, groups)
        for q in range(rows):
            greet(y_at[q] * line + z, gg)
        return carry

    lax.fori_loop(1, groups, greet_sheet, 0)

    lane = lax.broadcasted_iota(jnp.int32, (1, width), 1)
    lane_block = lane // bs
    lane_in = lane % bs
    row_at = lax.broadcasted_iota(jnp.int32, (bs, 1), 0)

    def masked(density, mask_ref):
        bound = jnp.zeros((1, width), jnp.int32)
        for k in range(7):
            gk, ak = shifted(*STEPS[k])
            value = sz_ref[gk, ak] * mask_ref[k, g, a] * exists(STEPS[k])
            bound = bound + jnp.where(lane_block == k, value, 0)
        keep_col = jnp.where(lane_in < bound, 1.0, 0.0)
        keep_row = jnp.where(row_at < sz_ref[g, a], 1.0, 0.0)
        return (density.astype(F32) * (keep_row * keep_col)).astype(BF16)

    for at in (1, 2, 3):
        loads[at].wait()
    vn[0] = masked(virt_ref[...], vm_ref)

    loads[0].wait()
    part = n_ao // 2
    n_rows = part * slab
    to = lax.broadcasted_iota(jnp.int32, (n_rows, n_rows), 0)
    frm = lax.broadcasted_iota(jnp.int32, (n_rows, n_rows), 1)
    perm = jnp.where(frm == (to % slab) * part + to // slab, 1.0, 0.0).astype(BF16)
    for half in range(2):
        rows_in = t_ref[:, half * part : (half + 1) * part, :].reshape(n_rows, width)
        moved_rows = jnp.dot(perm, rows_in, preferred_element_type=F32)
        snd[half * part : (half + 1) * part] = (
            moved_rows[:, :main].reshape(part, slab, main).astype(BF16)
        )
        for at in range(rows // 2):
            first = moved_rows[at * 2 * bs : at * 2 * bs + bs, main:]
            second = moved_rows[at * 2 * bs + bs : at * 2 * bs + 2 * bs, main:]
            y_out[half * (rows // 2) + at] = jnp.concatenate([first, second], axis=1).astype(BF16)

    pl.semaphore_wait(barrier, n_ao - 1 + (groups - 1) * rows)

    def v_copy(k):
        gk, ak = shifted(*(-x for x in STEPS[k]))
        return pltpu.make_async_remote_copy(
            src_ref=vn.at[0],
            dst_ref=vn.at[k],
            send_sem=v_send.at[k - 1],
            recv_sem=v_recv.at[k - 1],
            device_id={"ao": ak, "grp": gk},
            device_id_type=MESH,
        )

    def give_y(q):
        return pltpu.make_async_remote_copy(
            src_ref=y_out.at[y_at[q]],
            dst_ref=y_in.at[y],
            send_sem=y_send,
            recv_sem=y_recv,
            device_id={"ao": y_at[q] * line + z, "grp": g},
            device_id_type=MESH,
        )

    for q in range(rows - 1):
        give_y(q).start()

    def place_at(steps):
        return lax.rem(z + way * steps + line, line)

    def give(turn, z_to, z_block, count=rows):
        for q in range(count):
            pltpu.make_async_remote_copy(
                src_ref=snd.at[y_at[q] * line + z_block],
                dst_ref=arr.at[turn * rows + y],
                send_sem=a2a_send,
                recv_sem=a2a_recv.at[turn // (line // PARTS)],
                device_id={"ao": y_at[q] * line + z_to, "grp": g},
                device_id_type=MESH,
            ).start()

    def give_ahead(turn, carry):
        far = half_line - 1 - turn
        give(turn, place_at(-far), place_at(-far - 1))
        return carry

    def give_own(turn, carry):
        z_to = place_at(line - 1 - turn)
        give(turn, z_to, z_to)
        return carry

    v_copies = [v_copy(k) for k in range(1, 7)]
    for copy in v_copies:
        copy.start()
    lax.fori_loop(0, 4, give_ahead, 0)
    arr[(half_line - 1) * rows + y] = snd[y * line + place_at(-1)]
    arr[n_ao - rows + y] = snd[a]
    y_in[y] = y_out[y]

    for at in (4, 5, 6):
        loads[at].wait()
    occ = masked(occ_ref[...], om_ref)

    def wait_bytes(buf, count, sem):
        ref = buf.at[pl.ds(0, count - 1)]
        pltpu.make_async_copy(ref, ref, sem).wait()

    wait_bytes(y_in, rows, y_recv)
    for half in range(2):
        pieces = [y_in[at][:, half * bs : (half + 1) * bs].astype(F32) for at in range(rows)]
        upper = jnp.concatenate([pieces[0], pieces[2]], axis=1).reshape(line // 2, slab, 2 * bs)
        lower = jnp.concatenate([pieces[1], pieces[3]], axis=1).reshape(line // 2, slab, 2 * bs)
        z_out[half * (line // 2) : (half + 1) * (line // 2)] = jnp.concatenate(
            [upper, lower], axis=1
        ).astype(BF16)
    deep = 2 * slab

    def give_z(slot, turn, z_to, z_block):
        pltpu.make_async_remote_copy(
            src_ref=z_out.at[z_block],
            dst_ref=tt.at[slot, pl.ds(pl.multiple_of(turn * deep, deep), deep)],
            send_sem=z_send,
            recv_sem=z_recv.at[turn // (line // PARTS)],
            device_id={"ao": y * line + z_to, "grp": g},
            device_id_type=MESH,
        ).start()

    def give_z_ahead(turn, carry):
        far = half_line - 1 - turn
        give_z(4, turn, place_at(-far), place_at(-far - 1))
        return carry

    def give_z_own(turn, carry):
        z_to = place_at(line - 1 - turn)
        give_z(0, turn, z_to, z_to)
        return carry

    lax.fori_loop(0, half_line - 1, give_z_ahead, 0)
    lax.fori_loop(half_line, line - 1, give_z_own, 0)
    tt[4, (half_line - 1) * deep : half_line * deep] = z_out[place_at(-1)]
    tt[0, (line - 1) * deep : line * deep] = z_out[z]

    for copy in v_copies:
        copy.wait_recv()

    def towards(parity, axis):
        return (4 if parity == 0 else 3) if axis == 0 else (6 if parity == 0 else 5)

    def others(step):
        return [k for k in range(1, 7) if k != step]

    def block_of(value, k):
        return value[:, k * bs : (k + 1) * bs]

    for parity in range(2):

        @pl.when(odd == parity)
        def _(parity=parity):
            for axis in range(2):
                step = towards(parity, axis)
                for at, k in enumerate(others(step)):
                    here = block_of(vn[k], BACK[k])
                    there = block_of(occ if k == BACK[step] else vn[k], step)
                    pack[axis, at] = jnp.concatenate([here, there], axis=1)

    def along(axis, sign):
        return shifted(0, sign * way, 0) if axis == 0 else shifted(0, 0, sign * way)

    def p_copy(axis):
        gk, ak = along(axis, 1)
        return pltpu.make_async_remote_copy(
            src_ref=pack.at[axis],
            dst_ref=pack.at[2 + axis],
            send_sem=p_send.at[axis],
            recv_sem=p_recv.at[axis],
            device_id={"ao": ak, "grp": gk},
            device_id_type=MESH,
        )

    p_copies = [p_copy(axis) for axis in range(2)]
    for copy in p_copies:
        copy.start()
    lax.fori_loop(4, half_line - 1, give_ahead, 0)
    give(half_line - 1, z, place_at(-1), rows - 1)

    chunk = n_ao // PARTS
    high = chunk * slab

    def t_copy(to, p, lanes):
        source, target = 0, 1 + to
        if to < 2:
            gk, ak = shifted(1 - 2 * to, 0, 0)
        elif to == 3 and p < PARTS // 2:
            gk, ak = along(1, -1)
            source, target = target, source
        else:
            gk, ak = along(to - 2, 1)
        if lanes:
            here = tn.at[source, pl.ds(p * high, high), pl.ds(0, main)]
            there = tn.at[target, pl.ds(p * high, high), pl.ds(0, main)]
        else:
            here = tt.at[source, pl.ds(p * high // 2, high // 2)]
            there = tt.at[target, pl.ds(p * high // 2, high // 2)]
        return pltpu.make_async_remote_copy(
            src_ref=here,
            dst_ref=there,
            send_sem=ex_send.at[to, p, lanes],
            recv_sem=ex_recv.at[to, p, lanes],
            device_id={"ao": ak, "grp": gk},
            device_id_type=MESH,
        )

    t_copies = [[[t_copy(to, p, lanes) for lanes in range(2)] for p in range(PARTS)] for to in range(4)]

    def unpack_tail(at, p):
        last = tt[at, p * high // 2 : (p + 1) * high // 2, :].astype(F32)
        last = last.reshape(line // PARTS, deep, 2 * bs)
        both = jnp.concatenate([last[:, :, :bs], last[:, :, bs:]], axis=1)
        tn[at, p * high : (p + 1) * high, main:] = both.reshape(high, bs).astype(BF16)

    def take_part(p, slot, on_to):
        lacks = p % 2
        arrived = arr.at[pl.ds(p * chunk, chunk - lacks)]
        pltpu.make_async_copy(arrived, arrived, a2a_recv.at[p]).wait()
        tn[slot, p * high : (p + 1) * high, :main] = (
            arr[p * chunk : (p + 1) * chunk].astype(F32).reshape(high, main).astype(BF16)
        )
        for to in on_to:
            t_copies[to][p][1].start()
        arrived = tt.at[slot, pl.ds(p * high // 2, (line // PARTS - lacks) * deep)]
        pltpu.make_async_copy(arrived, arrived, z_recv.at[p]).wait()
        for to in on_to:
            t_copies[to][p][0].start()
        unpack_tail(slot, p)

    def pass_ahead_part(p):
        for lanes in (1, 0):
            t_copies[3][p][lanes].wait_recv()
            for to in (2, 1, 0):
                t_copies[to][p][lanes].start()
        unpack_tail(0, p)

    def mask_lanes(block_step):
        gi, ai = shifted(*block_step)
        on = jnp.zeros((1, width), jnp.int32)
        for j in range(7):
            value = tm_ref[j, gi, ai] * exists(block_step, STEPS[j])
            on = on + jnp.where(lane_block == j, value, 0)
        return on.astype(F32)

    own_lanes = mask_lanes(STEPS[0])
    nothing = jnp.zeros((bs, bs), F32)

    def place(slot, i, k, row_on, lanes_on, block):
        pieces = []
        for j in range(7):
            k2 = second_step(i, j, k)
            pieces.append(nothing if k2 is None else block(k2).astype(F32))
        placed = jnp.concatenate(pieces, axis=1) * lanes_on * row_on
        vs[slot, k * bs : (k + 1) * bs, :] = placed.astype(BF16)

    def place_all(slot_steps):
        lanes = [mask_lanes(STEPS[i]) for _, i in slot_steps]
        for k in range(7):
            row_on = (tm_ref[k, g, a] * exists(STEPS[k])).astype(F32)
            for (slot, i), lanes_on in zip(slot_steps, lanes):
                place(slot, i, k, row_on, lanes_on, lambda k2: block_of(vn[k], k2))

    lax.fori_loop(8, 10, give_own, 0)
    place_all([(0, 0), (1, 1), (2, 2)])
    for parity in range(2):

        @pl.when(odd == parity)
        def _(parity=parity):
            place_all([(3, BACK[towards(parity, 0)]), (4, BACK[towards(parity, 1)])])

    take_part(0, 4, (3,))
    lax.fori_loop(10, 12, give_own, 0)
    def source_of(slot, zz, ww):
        turn = slot >> 2
        ahead = jnp.where(turn < half_line, half_line - turn, turn - (line - 1))
        return (slot & (rows - 1)) * line + ((zz + ww * ahead + line) & (line - 1))

    def spread(zz, ww):
        down = lax.broadcasted_iota(jnp.int32, (tall, bs), 0) // slab
        across = lax.broadcasted_iota(jnp.int32, (bs, tall), 1) // slab
        tall_at = lax.broadcasted_iota(jnp.int32, (tall, bs), 1)
        wide_at = lax.broadcasted_iota(jnp.int32, (bs, tall), 0)
        as_rows = jnp.where(source_of(down, zz, ww) == tall_at, 1.0, 0.0).astype(BF16)
        as_cols = jnp.where(source_of(across, zz, ww) == wide_at, 1.0, 0.0).astype(BF16)
        return as_rows, as_cols

    own_rows, own_cols = spread(z, way)
    x_cols = spread(z, -way)[1]
    z_rows, z_cols = spread(place_at(-1), way)

    def weigh(slot, as_rows, block, as_cols):
        stretched = jnp.dot(as_rows, block, preferred_element_type=F32).astype(BF16)
        oexp[slot] = jnp.dot(stretched, as_cols, preferred_element_type=F32)

    def by_way(up, down):
        keep = odd.astype(F32)
        both = block_of(occ, up).astype(F32) * (1.0 - keep) + block_of(occ, down).astype(F32) * keep
        return both.astype(BF16)

    weigh(0, own_rows, block_of(occ, 0), own_cols)
    weigh(1, own_rows, block_of(occ, 1), x_cols)
    weigh(2, own_rows, block_of(occ, 2), x_cols)
    weigh(3, own_rows, by_way(3, 4), own_cols)
    weigh(4, own_rows, by_way(5, 6), z_cols)

    take_part(1, 4, (3,))
    lax.fori_loop(12, 15, give_own, 0)
    give(line - 1, z, z, rows - 1)
    for axis in range(2):
        p_copies[axis].wait_recv()
    for parity in range(2):

        @pl.when(odd == parity)
        def _(parity=parity):
            for axis in range(2):
                i = towards(parity, axis)
                ks = others(i)
                source = STEPS[BACK[i]]
                gs, a_s = shifted(*source)
                for k in range(7):
                    row_on = (tm_ref[k, gs, a_s] * exists(source, STEPS[k])).astype(F32)

                    def block(k2, k=k):
                        if k == 0:
                            return block_of(vn[BACK[i]], k2)
                        if k == i:
                            return block_of(vn[0], k2)
                        half = 0 if k2 == BACK[k] else 1
                        return block_of(pack[2 + axis, ks.index(k)], half)

                    place(5 + axis, i, k, row_on, own_lanes, block)
                received = pack[2 + axis, ks.index(BACK[i])]
                as_rows = own_rows if axis == 0 else z_rows
                weigh(5 + axis, as_rows, block_of(received, 1), own_cols)

    pass_ahead_part(0)
    take_part(2, 0, (3, 2, 1, 0))
    pass_ahead_part(1)
    take_part(3, 0, (3, 2, 1, 0))

    for s in range(5):
        xs[s] = jnp.dot(tn[0], vs[s], preferred_element_type=F32).astype(BF16)

    def pair_sum(slot, left, right, r0, r1_, c0, c1):
        pairs = lax.dot_general(left, right, (((1,), (1,)), ((), ())), preferred_element_type=F32)
        weighted = pairs * oexp[slot, r0:r1_, c0:c1]
        summed = jnp.sum(weighted.reshape((r1_ - r0) // slab, slab, c1 - c0), axis=0)
        folded = summed[:, 0:128]
        for at in range(1, (c1 - c0) // 128):
            folded = folded + summed[:, at * 128 : (at + 1) * 128]
        return folded

    part_sum = pair_sum(0, xs[0], tn[0], 0, tall, 0, tall)
    early = (PARTS - 1) * high
    for lo, hi, parts in ((0, early, range(PARTS - 1)), (early, tall, (PARTS - 1,))):
        for to in (0, 1, 2, 3):
            for p in parts:
                if to < 3 or p >= PARTS // 2:
                    for copy in t_copies[to][p]:
                        copy.wait_recv()
        for to in (0, 1, 2, 3):
            for p in parts:
                if to < 3 or p >= PARTS // 2:
                    unpack_tail(1 + to, p)
        both = {}
        for to in (2, 3):
            both[to] = jnp.dot(
                tn[1 + to, lo:hi, :], vs[3 + to], preferred_element_type=F32
            ).astype(BF16)
        for to in (0, 1, 2, 3):
            part_sum = part_sum + pair_sum(
                1 + to, xs[1 + to], tn[1 + to, lo:hi, :], 0, tall, lo, hi
            )
        for to in (2, 3):
            part_sum = part_sum + pair_sum(3 + to, both[to], tn[0], lo, hi, 0, tall)

    shift = 64
    while shift >= slab:
        part_sum = part_sum + pltpu.roll(part_sum, shift, 1)
        shift //= 2

    def left_all():
        for copy in v_copies + p_copies + [c for per in t_copies for two in per for c in two]:
            copy.wait_send()
        wait_bytes(snd, n_ao - 1, a2a_send)
        wait_bytes(y_out, rows, y_send)
        wait_bytes(z_out, line - 1, z_send)

    for p in range(slab):
        psend[p] = part_sum[p : p + 1, :]

    def all_slots(buf, count):
        acc = buf[0]
        for at in range(1, count):
            acc = acc + buf[at]
        return acc

    for dg in (4, 3, 5, 2, 6, 1, 7, 0):
        gg = lax.rem(g + dg, groups)
        for q in (1, 0, 2, 3):
            if dg or q < rows - 1:
                pltpu.make_async_remote_copy(
                    src_ref=psend.at[gg],
                    dst_ref=r1.at[g * rows + y],
                    send_sem=r_send.at[0],
                    recv_sem=r_recv.at[0],
                    device_id={"ao": y_at[q] * line + z, "grp": gg},
                    device_id_type=MESH,
                ).start()
    r1[g * rows + y] = psend[g]
    wait_bytes(r1, groups * rows, r_recv.at[0])
    r3[z] = all_slots(r1, groups * rows)

    def to_line(z_to):
        pltpu.make_async_remote_copy(
            src_ref=r3.at[z],
            dst_ref=r3.at[z],
            send_sem=r_send.at[1],
            recv_sem=r_recv.at[1],
            device_id={"ao": y * line + z_to, "grp": g},
            device_id_type=MESH,
        ).start()

    def to_both_ways(i, carry):
        for z_to, _ in both_ways(i):
            to_line(z_to)
        return carry

    to_line(across_line)
    lax.fori_loop(1, half_line, to_both_ways, 0)
    left_all()
    wait_bytes(r1, groups * rows, r_send.at[0])
    wait_bytes(r3, line, r_recv.at[1])
    scale = 1.0 / (bs * math.sqrt(groups * n_ao))
    out_ref[...] = (all_slots(r3, line) * scale)[:, :slab]
    wait_bytes(r3, line, r_send.at[1])


def body(three_center, occ_density, virt_density, tensor_mask, occ_mask, virt_mask, block_sizes):
    groups = lax.axis_size("grp")
    n_ao = lax.axis_size("ao")
    rows = 4
    line = n_ao // rows
    slab = three_center.shape[0]
    bs = occ_density.shape[2]
    width = 7 * bs
    tall = bs * slab
    dims = (groups, rows, line, slab, bs)
    dma = pltpu.SemaphoreType.DMA
    result = pl.pallas_call(
        functools.partial(kernel, dims),
        out_shape=jax.ShapeDtypeStruct((1, slab), F32),
        in_specs=[pl.BlockSpec(memory_space=pltpu.HBM)] * 7,
        out_specs=pl.BlockSpec(memory_space=pltpu.VMEM),
        scratch_shapes=[
            pltpu.VMEM((slab, n_ao, width), BF16),
            pltpu.VMEM((bs, width), BF16),
            pltpu.VMEM((bs, width), BF16),
            pltpu.SMEM((7, groups, n_ao), jnp.int32),
            pltpu.SMEM((7, groups, n_ao), jnp.int32),
            pltpu.SMEM((7, groups, n_ao), jnp.int32),
            pltpu.SMEM((groups, n_ao), jnp.int32),
            dma((7,)),
            pltpu.VMEM((n_ao, slab, width // 128 * 128), BF16),
            pltpu.VMEM((n_ao, slab, width // 128 * 128), BF16),
            pltpu.VMEM((5, tall, width), BF16),
            pltpu.VMEM((7, bs, width), BF16),
            pltpu.VMEM((4, 5, bs, 2 * bs), BF16),
            pltpu.VMEM((7, width, width), BF16),
            pltpu.VMEM((5, tall, width), BF16),
            pltpu.VMEM((7, tall, tall), F32),
            pltpu.VMEM((slab, 1, 128), F32),
            pltpu.VMEM((groups * rows, 1, 128), F32),
            pltpu.VMEM((line, 1, 128), F32),
            pltpu.VMEM((rows, bs, 2 * bs), BF16),
            pltpu.VMEM((rows, bs, 2 * bs), BF16),
            pltpu.VMEM((line, 2 * slab, 2 * bs), BF16),
            pltpu.VMEM((5, line * 2 * slab, 2 * bs), BF16),
            dma,
            dma((PARTS,)),
            dma,
            dma,
            dma,
            dma((PARTS,)),
            dma((4, PARTS, 2)),
            dma((4, PARTS, 2)),
            dma((6,)),
            dma((6,)),
            dma((2,)),
            dma((2,)),
            dma((2,)),
            dma((2,)),
        ],
        compiler_params=pltpu.CompilerParams(
            collective_id=0, has_side_effects=True, vmem_limit_bytes=60 * 1024 * 1024
        ),
    )(
        three_center,
        occ_density.reshape(bs, width),
        virt_density.reshape(bs, width),
        jnp.transpose(tensor_mask, (2, 0, 1)),
        jnp.transpose(occ_mask, (2, 0, 1)),
        jnp.transpose(virt_mask, (2, 0, 1)),
        block_sizes,
    )
    return result


def solution(mesh):
    in_specs = (
        P(None, "grp", "ao"),
        P("grp", "ao", None, None),
        P("grp", "ao", None, None),
        P(),
        P(),
        P(),
        P(),
    )
    return jax.shard_map(
        body, mesh=mesh, in_specs=in_specs, out_specs=P("grp", None), check_vma=False
    )
```
